32 devices in a mesh: beam: 2 (over x), wide: 16 (over z, y, core).
Axes of the slice: x: 2, y: 2, z: 4, core: 2. Of those that a mesh axis runs over, the one named last changes fastest.
Arguments:
- filterbank: bfloat16 [2, 4096, 4096], P('beam', 'wide'), parts along dimension 0, may hold values from -100 to 100
- channel_mask: int32 [8192], P(('beam', 'wide')), parts along dimension 0, may hold values 0 or 1
- band_edges: int32 [7], replicated, may hold values from 385 to 3711, as said below
- dm_delays: int32 [16], replicated, may hold values from 0 to 2047
Outputs:
- series: float32 [2, 16, 4096], P('beam', 'wide'), parts along dimension 0
The draws below stay inside these ranges and needn't reach their ends.
There are 2 independent parts, one for each index of `beam`. The reference program is written for one: setup_inputs(seed, part) draws one part's arguments, and reference() takes and returns one part's arrays. A program takes and returns all parts, laid end to end along the dimension named above; an argument that names none is the same for every part. Nothing has to cross between parts.
Inputs may be any that keep to these rules, and one draw needn't show every extreme that they name: `band_edges`: strictly increasing; entry i lies at (i + 1) * 512 up to a shift of less than 128.
All inputs are finite; a program needn't handle non-finite values. No bound on the sum of `channel_mask` on one device may be relied on, other than what follows from the above.
Results may differ from the reference program's by a relative error of at most 0.0063.
Values may be sent and summed in bfloat16 or wider, within the bound.
No kernel may reach another device: no remote copies, remote signals or barrier semaphores. Data moves between devices by JAX's collectives and lax.ppermute only.
A program may use at most 64 MiB of HBM per device.

```python
import math
import jax
import jax.numpy as jnp
from jax import lax

C = 4096
NT = 4096
NBLK = 8
NB = 1
NDM = 16
NBAND = 8


def draw_filterbank(key, part):
    key_noise, key_gain, key_time, key_ripple = jax.random.split(key, 4)
    channel_pos = jnp.arange(C, dtype=jnp.float32)
    ramp = 1.0 + 2.0 * channel_pos / (C - 1)
    offset = jax.random.uniform(key_ripple, (), minval=0.0, maxval=2.0 * math.pi)
    ripple = jnp.exp(jnp.sin(2.0 * math.pi * channel_pos * NBAND / (3.0 * C) + offset))
    noise = jax.random.normal(key_noise, (NB, C, NT))
    gain = jnp.exp(jax.random.uniform(key_gain, (C,)) * math.log(10.0))
    time_scale = jnp.exp(jax.random.uniform(key_time, (NB, 1, NT)) * math.log(10.0))
    values = noise * (ramp * ripple * gain)[None, :, None] * time_scale / 20.0
    return jnp.clip(values, -100.0, 100.0).astype(jnp.bfloat16)


def draw_band_edges(key, part):
    spacing = C // NBAND
    jitter = C // (4 * NBAND)
    offsets = jax.random.randint(key, (NBAND - 1,), -(jitter - 1), jitter)
    offsets = offsets.at[0].set(-(jitter - 1)).at[NBAND - 2].set(jitter - 1)
    return (jnp.arange(1, NBAND, dtype=jnp.int32) * spacing + offsets).astype(jnp.int32)


def plant(values, key, least, top_value):
    longest = values.shape.index(max(values.shape))
    spots = []
    for shift in (0, 1):
        where = [jax.random.randint(jax.random.fold_in(key, axis), (), 0, length) for axis, length in enumerate(values.shape)]
        where[longest] = (where[longest] + shift) % values.shape[longest]
        spots.append(tuple(where))
    return values.at[spots[0]].set(least).at[spots[1]].set(top_value)


def setup_inputs(seed: int = 0, part: int = 0) -> dict:
    seeds = jax.random.split(jax.random.key(seed), 5)
    own_keys = jax.random.split(jax.random.fold_in(seeds[4], part), 5)
    return {
        "filterbank": draw_filterbank(jax.random.fold_in(jax.random.fold_in(seeds[4], part), 71), part),
        "channel_mask": plant((jax.random.randint(own_keys[1], (C,), 0, 8) < 7).astype(jnp.int32), jax.random.fold_in(own_keys[1], 1), 0, 1),
        "band_edges": draw_band_edges(jax.random.fold_in(seeds[4], 71), part),
        "dm_delays": plant(jax.random.randint(seeds[3], (NDM,), 0, NT // 2), jax.random.fold_in(seeds[3], 1), 0, (NT // 2) - 1).astype(jnp.int32),
    }


def delay_fractions(first_channel, channel_count, total_channels):
    channel_ids = first_channel + jnp.arange(channel_count, dtype=jnp.int32)
    ratio = 0.5 + 0.5 * (channel_ids.astype(jnp.float32) + 0.5) / total_channels
    return (1.0 / (ratio * ratio) - 1.0) / 3.0

def noise_floors(band_power, band_edges, channels):
    bounds = jnp.concatenate([jnp.zeros((1,), jnp.int32), band_edges.astype(jnp.int32), jnp.full((1,), channels, jnp.int32)])
    widths = (bounds[1:] - bounds[:-1]).astype(jnp.float32)
    return jnp.sqrt(band_power / widths[None, :, None] + 1e-05)

def forward_tables(first_bin, bin_count, samples):
    bin_ids = first_bin + jnp.arange(bin_count, dtype=jnp.int32)
    times = jnp.arange(samples, dtype=jnp.int32)
    product = bin_ids[:, None] * times[None, :] % samples
    angle = product.astype(jnp.float32) * (2.0 * math.pi / samples)
    tables = jnp.stack([jnp.cos(angle), -jnp.sin(angle)], axis=0)
    return tables.reshape(2 * bin_count, samples).astype(jnp.bfloat16)

def inverse_tables(first_bin, bin_count, samples, channels):
    bin_ids = first_bin + jnp.arange(bin_count, dtype=jnp.int32)
    times = jnp.arange(samples, dtype=jnp.int32)
    product = bin_ids[:, None] * times[None, :] % samples
    angle = product.astype(jnp.float32) * (2.0 * math.pi / samples)
    weight = jnp.where(bin_ids == 0, 1.0, 2.0).astype(jnp.float32) / (samples * math.sqrt(channels))
    tables = jnp.stack([weight[:, None] * jnp.cos(angle), -weight[:, None] * jnp.sin(angle)], axis=1)
    return tables.reshape(2 * bin_count, samples).astype(jnp.bfloat16)

def phase_tables(first_bin, bin_count, fractions, dm_delays, samples):
    bin_ids = first_bin + jnp.arange(bin_count, dtype=jnp.int32)
    cycles = (bin_ids[:, None] * dm_delays[None, :]).astype(jnp.float32)
    angle = cycles[:, None, :] * fractions[None, :, None] * (2.0 * math.pi / samples)
    return (jnp.cos(angle).astype(jnp.bfloat16), jnp.sin(angle).astype(jnp.bfloat16))

def dedisperse_block(spec_real, spec_imag, cos_tab, sin_tab):
    spec_real = spec_real.astype(jnp.float32)
    spec_imag = spec_imag.astype(jnp.float32)
    cos_tab = cos_tab.astype(jnp.float32)
    sin_tab = sin_tab.astype(jnp.float32)
    real_part = jnp.einsum('fbc,fcd->fbd', spec_real, cos_tab) - jnp.einsum('fbc,fcd->fbd', spec_imag, sin_tab)
    imag_part = jnp.einsum('fbc,fcd->fbd', spec_real, sin_tab) + jnp.einsum('fbc,fcd->fbd', spec_imag, cos_tab)
    return jnp.stack([real_part, imag_part], axis=1)

def reference(filterbank, channel_mask, band_edges, dm_delays):
    beams, channels, samples = filterbank.shape
    bands = band_edges.shape[0] + 1
    signal = filterbank.astype(jnp.float32).reshape(beams, channels, NBLK, samples // NBLK)
    power = lax.optimization_barrier(jnp.mean(signal * signal, axis=3))
    channel_ids = jnp.arange(channels, dtype=jnp.int32)
    band_ids = lax.optimization_barrier(jnp.sum((band_edges[None, :] <= channel_ids[:, None]).astype(jnp.int32), axis=1))
    member = (band_ids[:, None] == jnp.arange(bands, dtype=jnp.int32)[None, :]).astype(jnp.float32)
    keep = channel_mask.astype(jnp.float32)
    band_power = jnp.einsum('cj,bck->bjk', member * keep[:, None], power, precision=lax.Precision.HIGHEST)
    floors = noise_floors(band_power, band_edges, channels)
    channel_floor = jnp.einsum('cj,bjk->bck', member, floors, precision=lax.Precision.HIGHEST)
    cleaned = (signal / channel_floor[..., None] * keep[None, :, None, None]).reshape(beams, channels, samples).astype(jnp.bfloat16)
    rows_flat = cleaned.reshape(beams * channels, samples)
    rows_turned = rows_flat.T
    bins = samples // 4
    dft_step = math.gcd(bins, 256)

    def spectrum_part(first_bin):
        tables = forward_tables(first_bin, dft_step, samples)
        block = jnp.dot(tables, rows_turned, preferred_element_type=jnp.float32).astype(jnp.bfloat16)
        return block.reshape(2, dft_step, beams, channels)
    firsts = jnp.arange(bins // dft_step, dtype=jnp.int32) * dft_step
    blocks = lax.map(spectrum_part, firsts)
    spectrum = jnp.transpose(blocks, (1, 0, 2, 3, 4)).reshape(2, bins, beams, channels)
    fractions = delay_fractions(0, channels, channels)
    phase_step = math.gcd(bins, 8)

    def dm_part(first_bin):
        spec_part = lax.dynamic_slice_in_dim(spectrum, first_bin, phase_step, 1)
        cos_tab, sin_tab = phase_tables(first_bin, phase_step, fractions, dm_delays, samples)
        return dedisperse_block(spec_part[0], spec_part[1], cos_tab, sin_tab)
    phase_firsts = jnp.arange(bins // phase_step, dtype=jnp.int32) * phase_step
    dm_blocks = lax.map(dm_part, phase_firsts)
    trials = dm_delays.shape[0]
    dm_spectrum = dm_blocks.reshape(bins, 2, beams, trials).astype(jnp.bfloat16)
    flat = dm_spectrum.reshape(bins * 2, beams * trials)
    table = inverse_tables(0, bins, samples, channels)
    series = jnp.dot(flat.T, table, preferred_element_type=jnp.float32)
    return series.reshape(beams, trials, samples)
```

```python
import functools
import math

import jax
import jax.numpy as jnp
import ml_dtypes
import numpy as np
from jax import lax
from jax.experimental import pallas as pl
from jax.experimental.pallas import tpu as pltpu
from jax.sharding import PartitionSpec as P

NBLK = 8
F32 = jnp.float32
BF16 = jnp.bfloat16
VMEM = pl.BlockSpec(memory_space=pltpu.VMEM)
SMEM = pl.BlockSpec(memory_space=pltpu.SMEM)
VMEM_BYTES = 48 * 2**20


def trig_coefficients(terms):
    n = 400
    y = 0.125 + 0.125 * np.cos(np.pi * (np.arange(n) + 0.5) / n)
    x = np.sqrt(y)
    out = []
    for values in (np.cos(2 * np.pi * x), np.sin(2 * np.pi * x) / x):
        fit = np.polynomial.Chebyshev.fit(y, values, terms - 1, domain=[0.0, 0.25])
        out.append([float(v) for v in fit.convert(kind=np.polynomial.Polynomial).coef])
    return out


def cos_sin_cycles(x):
    cos_c, sin_c = trig_coefficients(9)
    x = x - jnp.round(x)
    y = x * x
    c = jnp.full_like(x, cos_c[-1])
    s = jnp.full_like(x, sin_c[-1])
    for a, b in zip(cos_c[-2::-1], sin_c[-2::-1]):
        c = c * y + a
        s = s * y + b
    return c, s * x


def class_bins(r, bins):
    b = np.arange(bins // 64)[:, None]
    i = (np.arange(8)[None, :] - r) % 8
    return 64 * b + 8 * i + r


def forward_tables(samples):
    bins = samples // 4
    u = np.arange(samples // NBLK)

    def rows(r):
        f = class_bins(r, bins)[:, :, None]
        angle = 2.0 * np.pi * ((f * u) % samples) / samples
        return np.cos(angle), np.sin(angle)

    def put(real, imag):
        return np.stack([real, imag], axis=1).reshape(2 * bins // 8, -1)

    real_classes = []
    for r in (0, 4):
        c, s = rows(r)
        real_classes.append(put(c, -s))
    pairs = []
    for r in (1, 2, 3):
        c, s = rows(r)
        first = put(np.concatenate([c, s], -1), np.concatenate([-s, c], -1))
        c, s = rows(8 - r)
        second = put(np.concatenate([c, -s], -1), np.concatenate([-s, -c], -1))
        pairs.append(np.concatenate([first, second], 0))
    return (
        np.stack(real_classes).astype(ml_dtypes.bfloat16),
        np.stack(pairs).astype(ml_dtypes.bfloat16),
    )


def inverse_tables(samples, channels):
    bins = samples // 4
    g = np.arange(bins // 8)[:, None]
    q = np.arange(samples // 8)[None, :]
    angle = 2.0 * np.pi * ((8 * g * q) % samples) / samples
    first = np.concatenate([np.cos(angle), np.sin(angle)], 1).astype(ml_dtypes.bfloat16)
    r = np.arange(8)[:, None]
    weight = 2.0 / (samples * math.sqrt(channels))
    angle = 2.0 * np.pi * r * q / samples
    twiddle = (weight * np.stack([np.cos(angle), np.sin(angle)])).astype(np.float32)
    p = np.arange(8)[:, None]
    angle = 2.0 * np.pi * ((p * r.T) % 8) / 8
    last = np.concatenate([np.cos(angle), -np.sin(angle)], 1).astype(np.float32)
    return first, twiddle, last


def band_place(edges_ref, first, channels):
    band = jnp.int32(0)
    cut = jnp.int32(channels)
    for e in range(edges_ref.shape[0]):
        edge = edges_ref[e]
        band = band + (edge <= first).astype(jnp.int32)
        cut = jnp.where(edge > first, jnp.minimum(cut, edge), cut)
    return band, cut


def power_kernel(group, edges_ref, keep_ref, x_ref, out_ref, mask_ref):
    local = x_ref.shape[0]
    window = x_ref.shape[1] // NBLK
    first = lax.axis_index("wide") * local
    band, cut = band_place(edges_ref, first, local * group)
    ids = first + lax.broadcasted_iota(jnp.int32, (1, local), 1)
    keep = keep_ref[...].astype(F32)
    masks = []
    for j in range(2):
        inside = (ids < cut) if j == 0 else (ids >= cut)
        row = jnp.where(inside, keep, 0.0)
        column = jnp.broadcast_to(row, (128, local)).T
        mask_ref[j] = column
        masks.append(column)
    rows = []
    for k in range(NBLK):
        totals = [jnp.zeros((16, 128), F32) for _ in range(2)]
        for c in range(0, local, 16):
            squares = jnp.zeros((16, 128), F32)
            for u in range(k * window, (k + 1) * window, 128):
                v = x_ref[c : c + 16, u : u + 128].astype(F32)
                squares = squares + v * v
            for j in range(2):
                totals[j] = totals[j] + squares * mask_ref[j, c : c + 16, :]
        rows.append(totals)
    flat = jnp.concatenate(
        [jnp.sum(rows[k][j], axis=0, keepdims=True) for j in range(2) for k in range(NBLK)], axis=0
    )
    sums = jnp.sum(flat, axis=1, keepdims=True) * (1.0 / window)
    lanes = out_ref.shape[1]
    lane = lax.broadcasted_iota(jnp.int32, (2 * NBLK, lanes), 1)
    row = lax.broadcasted_iota(jnp.int32, (2 * NBLK, lanes), 0)
    placed = jnp.where(lane == band * NBLK + row, jnp.broadcast_to(sums, lane.shape), 0.0)
    out_ref[...] = jnp.broadcast_to(jnp.sum(placed, axis=0, keepdims=True), out_ref.shape)


def phase_kernel(channels, samples, delays_ref, base_ref, turn_ref, step_ref):
    local, lanes = base_ref.shape[1:]
    first = lax.axis_index("wide") * local
    lane = lax.broadcasted_iota(jnp.int32, (8, lanes), 1)
    delay = jnp.zeros((8, lanes), F32)
    for d in range(delays_ref.shape[0]):
        delay = jnp.where((lane >> 3) == d, delays_ref[d].astype(F32), delay)
    start = (3.5 + 8.0 * (lane & 7).astype(F32)) * delay

    def rows(n, carry):
        c = pl.multiple_of(n * 8, 8)
        channel = first + c + lax.broadcasted_iota(jnp.int32, (8, lanes), 0)
        ratio = 0.5 + 0.5 * (channel.astype(F32) + 0.5) / channels
        fraction = (1.0 / (ratio * ratio) - 1.0) / 3.0 / samples
        at = pl.ds(c, 8)
        base_ref[0, at, :], base_ref[1, at, :] = cos_sin_cycles(start * fraction)
        turn_ref[0, at, :], turn_ref[1, at, :] = cos_sin_cycles((64.0 * delay) * fraction)
        for j in range(4):
            step_ref[j, 0, at, :], step_ref[j, 1, at, :] = cos_sin_cycles(((j + 0.5) * delay) * fraction)
        return carry

    lax.fori_loop(0, local // 8, rows, 0, unroll=2)


def window_classes(y):
    half = math.sqrt(0.5)
    e = [y[k] + y[k + 4] for k in range(4)]
    o = [y[k] - y[k + 4] for k in range(4)]
    a, b = e[0] + e[2], e[1] + e[3]
    p, q = half * (o[1] - o[3]), half * (o[1] + o[3])
    return [a + b, a - b, o[0] + p, -(o[2] + q), e[0] - e[2], e[3] - e[1], o[0] - p, o[2] - q]


def main_kernel(
    group, edges_ref, x_ref, power_ref, mask_ref, base_ref, turn_ref, step_ref, real_ref, pair_ref,
    out_ref, z_ref, spec_ref, even_ref, odd_ref, state_ref, part_ref,
):
    local, samples = x_ref.shape
    window = samples // NBLK
    lanes = base_ref.shape[2]
    first = lax.axis_index("wide") * local
    channels = local * group
    band, _ = band_place(edges_ref, first, channels)

    power = jnp.sum(power_ref[...], axis=0, keepdims=True)
    wide = power.shape[1]
    lane = lax.broadcasted_iota(jnp.int32, (1, wide), 1)
    width = jnp.ones((1, wide), F32)
    edges = edges_ref.shape[0]
    for j in range(edges + 1):
        low = edges_ref[j - 1] if j else jnp.int32(0)
        high = edges_ref[j] if j < edges else jnp.int32(channels)
        width = jnp.where((lane >> 3) == j, (high - low).astype(F32), width)
    floor = jnp.sqrt(power / width + 1e-05)
    inverse = jnp.broadcast_to(1.0 / floor, (8, wide))
    inverse = pltpu.roll(inverse, (wide - band * NBLK) % wide, 1)
    scale = [
        [jnp.broadcast_to(inverse[:, j * NBLK + k : j * NBLK + k + 1], (8, 128)) for k in range(NBLK)]
        for j in range(2)
    ]
    scale = [[jnp.concatenate([v, v], axis=0) for v in row] for row in scale]

    def combine(n, carry):
        c = pl.ds(pl.multiple_of(n * 16, 16), 16)
        m0, m1 = mask_ref[0, c, :], mask_ref[1, c, :]
        weight = [m0 * scale[0][k] + m1 * scale[1][k] for k in range(NBLK)]
        for u in range(0, window, 128):
            y = [x_ref[c, k * window + u : k * window + u + 128].astype(F32) * weight[k] for k in range(NBLK)]
            for n_out, z in enumerate(window_classes(y)):
                z_ref[c, n_out * window + u : n_out * window + u + 128] = z.astype(BF16)
        return carry

    lax.fori_loop(0, local // 16, combine, 0, unroll=2)

    rows = spec_ref.shape[1]
    contract = (((1,), (1,)), ((), ()))
    for n, r in enumerate((0, 4)):
        spec_ref[r] = lax.dot_general(
            real_ref[n], z_ref[:, n * window : (n + 1) * window], contract, preferred_element_type=F32
        ).astype(BF16)
    for n in range(3):
        z = z_ref[:, 2 * (n + 1) * window : 2 * (n + 2) * window]
        for r, at in ((n + 1, 0), (7 - n, rows)):
            spec_ref[r] = lax.dot_general(
                pair_ref[n, at : at + rows, :], z, contract, preferred_element_type=F32
            ).astype(BF16)

    sub = lax.broadcasted_iota(jnp.int32, (8, lanes), 0)
    inner = lax.broadcasted_iota(jnp.int32, (8, lanes), 1) & 7
    skew = (sub - inner) & 7
    state_ref[...] = base_ref[...]

    def phases(e_ref):
        for c in range(0, local, 16):
            at = slice(c, c + 16)
            cos0, sin0 = state_ref[0, at, :], state_ref[1, at, :]
            for j in range(4):
                cos_j, sin_j = step_ref[j, 0, at, :], step_ref[j, 1, at, :]
                cc, ss, sc, cs = cos0 * cos_j, sin0 * sin_j, sin0 * cos_j, cos0 * sin_j
                e_ref[4 + j, at, :lanes] = (cc - ss).astype(BF16)
                e_ref[4 + j, at, lanes:] = (sc + cs).astype(BF16)
                e_ref[3 - j, at, :lanes] = (cc + ss).astype(BF16)
                e_ref[3 - j, at, lanes:] = (sc - cs).astype(BF16)
            cos_t, sin_t = turn_ref[0, at, :], turn_ref[1, at, :]
            state_ref[0, at, :] = cos0 * cos_t - sin0 * sin_t
            state_ref[1, at, :] = sin0 * cos_t + cos0 * sin_t

    def dedisperse(b, e_ref):
        at = pl.ds(pl.multiple_of(b * 16, 16), 16)
        real = imag = None
        for r in range(8):
            o = jnp.dot(spec_ref[r, at, :], e_ref[r], preferred_element_type=F32)
            re = o[0:8, :lanes] - o[8:16, lanes:]
            im = o[0:8, lanes:] + o[8:16, :lanes]
            real = re if r == 0 else jnp.where(skew == r, re, real)
            imag = im if r == 0 else jnp.where(skew == r, im, imag)
        for bit in (1, 2, 4):
            move = (inner & bit) != 0
            real = jnp.where(move, pltpu.roll(real, 8 - bit, 0), real)
            imag = jnp.where(move, pltpu.roll(imag, 8 - bit, 0), imag)
        part_ref[0, b] = real
        part_ref[1, b] = imag

    phases(even_ref)

    def pair(n, carry):
        phases(odd_ref)
        dedisperse(2 * n, even_ref)
        phases(even_ref)
        dedisperse(2 * n + 1, odd_ref)
        return carry

    blocks = part_ref.shape[1]
    lax.fori_loop(0, blocks // 2, pair, 0)

    block = lax.broadcasted_iota(jnp.int32, (8, 128), 1) >> 3
    for half in range(lanes // 128):
        done = []
        for part in range(2):
            v = [part_ref[part, b, :, half * 128 : half * 128 + 128] for b in range(16)]
            for bit in (1, 2, 4, 8):
                w = list(v)
                high = (block & bit) != 0
                for b in range(16):
                    if b & bit:
                        w[b] = jnp.where(high, v[b], pltpu.roll(v[b ^ bit], 128 - 8 * bit, 1))
                    else:
                        w[b] = jnp.where(high, pltpu.roll(v[b ^ bit], 8 * bit, 1), v[b])
                v = w
            done.append(v)
        for d in range(16):
            out_ref[half * 16 + d] = jnp.concatenate([done[0][d], done[1][d]], axis=0).astype(BF16)


def inverse_kernel(group, got_ref, first_ref, twiddle_ref, last_ref, out_ref):
    step = first_ref.shape[1] // 2
    trials = out_ref.shape[1]
    row = lax.broadcasted_iota(jnp.int32, (16, 128), 0)
    lane = lax.broadcasted_iota(jnp.int32, (16, 128), 1)
    dc = ((row & 7) == 0) & (lane == 0)
    for d in range(trials):
        total = got_ref[d].astype(F32)
        for n in range(1, group):
            total = total + got_ref[n * trials + d].astype(F32)
        total = jnp.where(dc, 0.5 * total, total).astype(BF16)
        y = jnp.dot(total, first_ref[...], preferred_element_type=F32)
        real = y[0:8, :step] - y[8:16, step:]
        imag = y[0:8, step:] + y[8:16, :step]
        cos, sin = twiddle_ref[0], twiddle_ref[1]
        z = jnp.concatenate([real * cos - imag * sin, real * sin + imag * cos], axis=0)
        series = jnp.dot(last_ref[...], z, precision=lax.Precision.HIGHEST, preferred_element_type=F32)
        for p in range(8):
            out_ref[0, d : d + 1, p * step : (p + 1) * step] = series[p : p + 1, :]


def call(kernel, out_shape, in_specs, scratch=(), name=None):
    return pl.pallas_call(
        kernel,
        out_shape=out_shape,
        in_specs=in_specs,
        out_specs=jax.tree.map(lambda _: VMEM, out_shape),
        scratch_shapes=list(scratch),
        compiler_params=pltpu.CompilerParams(vmem_limit_bytes=VMEM_BYTES),
        name=name,
    )


def body(filterbank, channel_mask, band_edges, dm_delays):
    _, local, samples = filterbank.shape
    group = lax.axis_size("wide")
    channels = local * group
    trials = dm_delays.shape[0]
    lanes = 8 * trials
    bins = samples // 4
    blocks = bins // 64
    shape = jax.ShapeDtypeStruct
    x = filterbank.reshape(local, samples)
    power_lanes = -(-(band_edges.shape[0] + 1) * NBLK // 128) * 128

    power, masks = call(
        functools.partial(power_kernel, group),
        (shape((group, power_lanes), F32), shape((2, local, 128), F32)),
        [SMEM, VMEM, VMEM],
        name="band_power",
    )(band_edges, channel_mask.reshape(1, local), x)
    all_power = lax.all_to_all(power, "wide", 0, 0, tiled=True)

    base, turn, step = call(
        functools.partial(phase_kernel, channels, samples),
        (shape((2, local, lanes), F32), shape((2, local, lanes), F32), shape((4, 2, local, lanes), F32)),
        [SMEM],
        name="phase_steps",
    )(dm_delays)

    real_table, pair_table = forward_tables(samples)
    partial = call(
        functools.partial(main_kernel, group),
        shape((trials, 16, 128), BF16),
        [SMEM] + [VMEM] * 8,
        [
            pltpu.VMEM((local, samples), BF16),
            pltpu.VMEM((8, bins // 4, local), BF16),
            pltpu.VMEM((8, local, 2 * lanes), BF16),
            pltpu.VMEM((8, local, 2 * lanes), BF16),
            pltpu.VMEM((2, local, lanes), F32),
            pltpu.VMEM((2, blocks, 8, lanes), F32),
        ],
        name="dedisperse",
    )(band_edges, x, all_power, masks, base, turn, step, jnp.asarray(real_table), jnp.asarray(pair_table))
    got = lax.all_to_all(partial, "wide", 0, 0, tiled=True)

    first, twiddle, last = inverse_tables(samples, channels)
    return call(
        functools.partial(inverse_kernel, group),
        shape((1, trials // group, samples), F32),
        [VMEM] * 4,
        name="inverse",
    )(got, jnp.asarray(first), jnp.asarray(twiddle), jnp.asarray(last))


def solution(mesh):
    return jax.shard_map(
        body,
        mesh=mesh,
        in_specs=(P("beam", "wide", None), P(("beam", "wide")), P(), P()),
        out_specs=P("beam", "wide", None),
        check_vma=False,
    )
```

```python
import functools
import math

import jax
import jax.numpy as jnp
import ml_dtypes
import numpy as np
from jax import lax
from jax.experimental import pallas as pl
from jax.experimental.pallas import tpu as pltpu
from jax.sharding import PartitionSpec as P

NBLK = 8
HEAD = 3 * NBLK
LATE = (0, 1)
F32 = jnp.float32
BF16 = jnp.bfloat16
VMEM = pl.BlockSpec(memory_space=pltpu.VMEM)
HBM = pl.BlockSpec(memory_space=pltpu.HBM)


def trig_coefficients(terms):
    n = 400
    y = 0.125 + 0.125 * np.cos(np.pi * (np.arange(n) + 0.5) / n)
    x = np.sqrt(y)
    out = []
    for values in (np.cos(2 * np.pi * x), np.sin(2 * np.pi * x) / x):
        fit = np.polynomial.Chebyshev.fit(y, values, terms - 1, domain=[0.0, 0.25])
        out.append([float(v) for v in fit.convert(kind=np.polynomial.Polynomial).coef])
    return out


def cos_sin_cycles(x):
    cos_c, sin_c = trig_coefficients(9)
    x = x - jnp.round(x)
    y = x * x
    c = jnp.full_like(x, cos_c[-1])
    s = jnp.full_like(x, sin_c[-1])
    for a, b in zip(cos_c[-2::-1], sin_c[-2::-1]):
        c = c * y + a
        s = s * y + b
    return c, s * x


def class_bins(r, bins):
    b = np.arange(bins // 64)[:, None]
    i = (np.arange(8)[None, :] - r) % 8
    return 64 * b + 8 * i + r


def forward_tables(samples):
    bins = samples // 4
    u = np.arange(samples // NBLK)
    tables = []
    for r in range(8):
        f = class_bins(r, bins)[:, :, None]
        angle = 2.0 * np.pi * ((f * u) % samples) / samples
        tables.append(np.stack([np.cos(angle), -np.sin(angle)]).reshape(bins // 4, -1))
    return np.concatenate(tables, 0).astype(ml_dtypes.bfloat16)


def inverse_tables(samples, channels):
    bins = samples // 4
    g = np.arange(bins // 8)[:, None]
    q = np.arange(samples // 8)[None, :]
    angle = 2.0 * np.pi * ((8 * g * q) % samples) / samples
    exact = np.concatenate([np.cos(angle), np.sin(angle)], 1)
    high = exact.astype(ml_dtypes.bfloat16)
    first = np.stack([high, (exact - high.astype(np.float64)).astype(ml_dtypes.bfloat16)])
    r = np.arange(8)[:, None]
    weight = 2.0 / (samples * math.sqrt(channels))
    angle = 2.0 * np.pi * r * q / samples
    twiddle = (weight * np.stack([np.cos(angle), np.sin(angle)])).astype(np.float32)
    p = np.arange(8)[:, None]
    angle = 2.0 * np.pi * ((p * r.T) % 8) / 8
    last = np.concatenate([np.cos(angle), -np.sin(angle)], 1).astype(np.float32)
    return first, twiddle, last


def band_place(edges_ref, first, channels):
    band = jnp.int32(0)
    cut = jnp.int32(channels)
    for e in range(edges_ref.shape[0]):
        edge = edges_ref[e]
        band = band + (edge <= first).astype(jnp.int32)
        cut = jnp.where(edge > first, jnp.minimum(cut, edge), cut)
    return band, cut


def power_kernel(
    group, edges_hbm, keep_hbm, delays_hbm, x_hbm, out_ref, info_ref,
    x_ref, mask_ref, edges_ref, keep_ref, delays_ref, sems, x_sems,
):
    local = x_ref.shape[0]
    window = x_ref.shape[1] // NBLK
    parts = x_sems.shape[0]
    step = local // parts
    channels = local * group
    small = [
        pltpu.make_async_copy(source, target, sems.at[n])
        for n, (source, target) in enumerate(((edges_hbm, edges_ref), (keep_hbm, keep_ref), (delays_hbm, delays_ref)))
    ]
    large = [
        pltpu.make_async_copy(x_hbm.at[pl.ds(n * step, step)], x_ref.at[pl.ds(n * step, step)], x_sems.at[n])
        for n in range(parts)
    ]
    for copy in small + large:
        copy.start()
    for copy in small:
        copy.wait()
    first = lax.axis_index("wide") * local
    band = jnp.int32(0)
    cut = jnp.int32(channels)
    edges = edges_ref.shape[0]
    for e in range(edges):
        edge = edges_ref[e]
        band = band + (edge <= first).astype(jnp.int32)
        cut = jnp.where(edge > first, jnp.minimum(cut, edge), cut)
    ids = first + lax.broadcasted_iota(jnp.int32, (1, local), 1)
    keep = keep_ref[...].astype(F32)
    masks = [jnp.where(inside, keep, 0.0) for inside in (ids < cut, ids >= cut)]
    for j in range(2):
        mask_ref[j] = jnp.broadcast_to(masks[j], (128, local)).T

    wide = info_ref.shape[1]
    lane = lax.broadcasted_iota(jnp.int32, (2 * NBLK, wide), 1)
    row = lax.broadcasted_iota(jnp.int32, (2 * NBLK, wide), 0)
    place = lane == band * NBLK + row
    info_ref[: 2 * NBLK, :] = jnp.where(place, 1.0, 0.0)
    width = jnp.ones((8, wide), F32)
    for j in range(edges + 1):
        low = edges_ref[j - 1] if j else jnp.int32(0)
        high = edges_ref[j] if j < edges else jnp.int32(channels)
        width = jnp.where((lane[:8] >> 3) == j, (high - low).astype(F32), width)
    info_ref[2 * NBLK : HEAD, :] = width
    delay = jnp.zeros((8, wide), F32)
    for d in range(delays_ref.shape[0]):
        delay = jnp.where((lane[:8] >> 3) == d, delays_ref[d].astype(F32), delay)
    info_ref[HEAD:, :] = delay
    for j in range(2):
        info_ref[HEAD + j : HEAD + j + 1, :local] = masks[j]

    totals = [[jnp.zeros((16, 128), F32) for _ in range(NBLK)] for _ in range(2)]
    for n in range(parts):
        large[n].wait()
        for c in range(n * step, (n + 1) * step, 16):
            for k in range(NBLK):
                squares = jnp.zeros((16, 128), F32)
                for u in range(k * window, (k + 1) * window, 128):
                    v = x_ref[c : c + 16, u : u + 128].astype(F32)
                    squares = squares + v * v
                for j in range(2):
                    totals[j][k] = totals[j][k] + squares * mask_ref[j, c : c + 16, :]
    flat = jnp.concatenate([jnp.sum(t, axis=0, keepdims=True) for row in totals for t in row], axis=0)
    sums = jnp.sum(flat, axis=1, keepdims=True) * (1.0 / window)
    lanes = out_ref.shape[1]
    placed = jnp.where(place[:, :lanes], jnp.broadcast_to(sums, (2 * NBLK, lanes)), 0.0)
    out_ref[...] = jnp.broadcast_to(jnp.sum(placed, axis=0, keepdims=True), out_ref.shape)


def turned(a, b):
    return a[0] * b[0] - a[1] * b[1], a[1] * b[0] + a[0] * b[1]


def phase_kernel(group, info_ref, x_hbm, pack_ref, x_ref, sem):
    local, samples = x_ref.shape
    lanes = pack_ref.shape[1]
    channels = local * group
    copy = pltpu.make_async_copy(x_hbm, x_ref, sem)
    copy.start()
    first = lax.axis_index("wide") * local
    pack_ref[:HEAD, :] = info_ref[:HEAD, :lanes]
    for j in range(2):
        mask = jnp.broadcast_to(info_ref[HEAD + j : HEAD + j + 1, :local], (lanes, local))
        pack_ref[HEAD + j * local : HEAD + (j + 1) * local, :] = mask.T
    lane = lax.broadcasted_iota(jnp.int32, (16, lanes), 1)
    delay = jnp.broadcast_to(info_ref[HEAD + 2 : HEAD + 3, :lanes], (16, lanes))
    bins = ((3.5 + 8.0 * (lane & 7).astype(F32)) * delay, 64.0 * delay, 0.5 * delay)

    def rows(n, carry):
        c = pl.multiple_of(n * 16, 16)
        channel = first + c + lax.broadcasted_iota(jnp.int32, (16, lanes), 0)
        ratio = 0.5 + 0.5 * (channel.astype(F32) + 0.5) / channels
        fraction = (1.0 / (ratio * ratio) - 1.0) / 3.0 / samples
        for m in range(3):
            for q, v in enumerate(cos_sin_cycles(bins[m] * fraction)):
                pack_ref[pl.ds(pl.multiple_of(HEAD + (2 + 2 * m + q) * local + c, 8), 16), :] = v
        return carry

    lax.fori_loop(0, local // 16, rows, 0, unroll=2)
    copy.wait()


def window_classes(y):
    half = math.sqrt(0.5)
    e = [y[k] + y[k + 4] for k in range(4)]
    o = [y[k] - y[k + 4] for k in range(4)]
    a, b = e[0] + e[2], e[1] + e[3]
    p, q = half * (o[1] - o[3]), half * (o[1] + o[3])
    return [a + b, a - b, o[0] + p, -(o[2] + q), e[0] - e[2], e[3] - e[1], o[0] - p, o[2] - q]


def main_kernel(
    power_ref, x_ref, pack_ref, table_hbm,
    out_ref, table_ref, z_ref, spec_ref, state_ref, step_ref, part_ref, table_sems,
):
    local, samples = x_ref.shape
    window = samples // NBLK
    lanes = pack_ref.shape[1]
    rows = table_ref.shape[0] // 8
    head = HEAD + 2 * local
    table_copies = [
        pltpu.make_async_copy(
            table_hbm.at[pl.ds(n * rows, rows)], table_ref.at[pl.ds(n * rows, rows)], table_sems.at[n]
        )
        for n in range(8)
    ]
    for copy in table_copies:
        copy.start()
    power = jnp.sum(power_ref[...], axis=0, keepdims=True)
    wide = power.shape[1]
    inverse = 1.0 / jnp.sqrt(power / pack_ref[2 * NBLK : 2 * NBLK + 1, :wide] + 1e-05)
    column = jnp.sum(pack_ref[: 2 * NBLK, :wide] * inverse, axis=1, keepdims=True)
    column = jnp.broadcast_to(column, (2 * NBLK, 128))
    scale = [
        [jnp.broadcast_to(column[j * NBLK + k : j * NBLK + k + 1, :], (16, 128)) for k in range(NBLK)]
        for j in range(2)
    ]

    waiting = []

    def store(next_stores):
        for ref, index, value in waiting:
            ref[index] = value
        waiting[:] = next_stores

    for c in range(0, local, 16):
        at = slice(c, c + 16)
        m0 = pack_ref[HEAD + c : HEAD + c + 16, :128]
        m1 = pack_ref[HEAD + local + c : HEAD + local + c + 16, :128]
        weight = [m0 * scale[0][k] + m1 * scale[1][k] for k in range(NBLK)]
        for u in range(0, window, 128):
            y = [x_ref[at, k * window + u : k * window + u + 128].astype(F32) * weight[k] for k in range(NBLK)]
            classes = window_classes(y)
            classes += [-classes[m] for m in (3, 5, 7)]
            store([
                (z_ref, (at, slice(m * window + u, m * window + u + 128)), z.astype(BF16))
                for m, z in enumerate(classes)
            ])
    store([])

    blocks = rows // 16
    contract = (((1,), (1,)), ((), ()))

    def put(r, real, imag):
        j, at = (r - 4, 0) if r >= 4 else (3 - r, 16)
        both = jnp.concatenate([v.reshape(blocks, 8, local) for v in (real, imag)], axis=1)
        spec_ref[j, :, at : at + 16, :] = both.astype(BF16)

    def across(table, n):
        return lax.dot_general(table, n, contract, preferred_element_type=F32)

    half = rows // 2
    for r in (0, 4):
        table_copies[r].wait()
        at = r // 4 * window
        found = across(table_ref[r * rows : (r + 1) * rows, :], z_ref[:, at : at + window])
        put(r, found[:half], found[half:])
    for r in (1, 2, 3):
        table_copies[r].wait()
        table_copies[8 - r].wait()
        real, imag, minus = (z_ref[:, n * window : (n + 1) * window] for n in (2 * r, 2 * r + 1, 7 + r))
        (cos_a, sin_a), (cos_b, sin_b) = (
            (table_ref[n * rows : n * rows + half, :], table_ref[n * rows + half : (n + 1) * rows, :]) for n in (r, 8 - r)
        )
        left = [jnp.concatenate(pair, axis=1) for pair in ((sin_a, cos_a), (cos_b, sin_b))]
        plus = across(jnp.concatenate(left, axis=0), jnp.concatenate([real, imag], axis=1))
        left = [jnp.concatenate(pair, axis=1) for pair in ((cos_a, sin_a), (sin_b, cos_b))]
        other = across(jnp.concatenate(left, axis=0), jnp.concatenate([real, minus], axis=1))
        put(r, other[:half], plus[:half])
        put(8 - r, plus[half:], other[half:])

    def phase(m, at):
        return pack_ref[head + m * local + at.start : head + m * local + at.stop, :]

    for c in range(0, local, 16):
        at = slice(c, c + 16)
        step = phase(4, at), phase(5, at)
        one = turned(step, step)
        stores = [(state_ref, (q, at, slice(None)), phase(q, at)) for q in range(2)]
        for j in range(4):
            stores += [(step_ref, (j, q, at, slice(None)), step[q]) for q in range(2)]
            step = turned(step, one)
        store(stores)
    store([])

    sub = lax.broadcasted_iota(jnp.int32, (8, lanes), 0)
    inner = lax.broadcasted_iota(jnp.int32, (8, lanes), 1) & 7
    skew = (sub - inner) & 7

    def dedisperse(b, carry):
        made = []
        for c in range(0, local, 16):
            at = slice(c, c + 16)
            state = cos0, sin0 = state_ref[0, at, :], state_ref[1, at, :]
            products = []
            for j in range(4):
                cos_j, sin_j = step_ref[j, 0, at, :], step_ref[j, 1, at, :]
                cc, ss, sc, cs = cos0 * cos_j, sin0 * sin_j, sin0 * cos_j, cos0 * sin_j
                pairs = ((cc, ss), (sc, cs)) if j in LATE else ((cc - ss, sc + cs), (cc + ss, sc - cs))
                for pair in pairs:
                    products.append(jnp.concatenate([v.astype(BF16) for v in pair], axis=1))
            made.append(products)
            moved = turned(state, (phase(2, at), phase(3, at)))
            store([(state_ref, (q, at, slice(None)), moved[q]) for q in range(2)])
        store([])
        tiles = [jnp.concatenate([products[n] for products in made], axis=0) for n in range(8)]
        found = [None] * 8
        for j in range(4):
            both = spec_ref[j, b]
            if j in LATE:
                p = jnp.dot(both, tiles[2 * j], preferred_element_type=F32)
                q = jnp.dot(both, tiles[2 * j + 1], preferred_element_type=F32)
                up, down = slice(0, 16), slice(16, 32)
                cos_up, sin_up = p[up, :lanes] - p[up, lanes:], q[up, :lanes] + q[up, lanes:]
                cos_down, sin_down = p[down, :lanes] + p[down, lanes:], q[down, :lanes] - q[down, lanes:]
            else:
                up = jnp.dot(both[:16], tiles[2 * j], preferred_element_type=F32)
                down = jnp.dot(both[16:], tiles[2 * j + 1], preferred_element_type=F32)
                cos_up, sin_up, cos_down, sin_down = up[:, :lanes], up[:, lanes:], down[:, :lanes], down[:, lanes:]
            found[4 + j] = cos_up[:8] - sin_up[8:], sin_up[:8] + cos_up[8:]
            found[3 - j] = cos_down[:8] - sin_down[8:], sin_down[:8] + cos_down[8:]
        real, imag = found[0]
        for r in range(1, 8):
            real = jnp.where(skew == r, found[r][0], real)
            imag = jnp.where(skew == r, found[r][1], imag)
        for bit in (1, 2, 4):
            move = (inner & bit) != 0
            real = jnp.where(move, pltpu.roll(real, 8 - bit, 0), real)
            imag = jnp.where(move, pltpu.roll(imag, 8 - bit, 0), imag)
        part_ref[0, b] = real
        part_ref[1, b] = imag
        return carry

    lax.fori_loop(0, blocks, dedisperse, 0, unroll=4)

    block = lax.broadcasted_iota(jnp.int32, (8, 128), 1) >> 3
    for half in range(lanes // 128):
        done = []
        for part in range(2):
            v = [part_ref[part, b, :, half * 128 : half * 128 + 128] for b in range(16)]
            for bit in (1, 2, 4, 8):
                w = list(v)
                high = (block & bit) != 0
                for b in range(16):
                    if b & bit:
                        w[b] = jnp.where(high, v[b], pltpu.roll(v[b ^ bit], 128 - 8 * bit, 1))
                    else:
                        w[b] = jnp.where(high, pltpu.roll(v[b ^ bit], 8 * bit, 1), v[b])
                v = w
            done.append(v)
        for d in range(16):
            out_ref[half * 16 + d] = jnp.concatenate([done[0][d], done[1][d]], axis=0).astype(BF16)


def inverse_kernel(group, got_ref, first_ref, twiddle_ref, last_ref, out_ref):
    step = first_ref.shape[2] // 2
    trials = out_ref.shape[1]
    row = lax.broadcasted_iota(jnp.int32, (16, 128), 0)
    lane = lax.broadcasted_iota(jnp.int32, (16, 128), 1)
    dc = ((row & 7) == 0) & (lane == 0)
    for d in range(trials):
        total = got_ref[d].astype(F32)
        for n in range(1, group):
            total = total + got_ref[n * trials + d].astype(F32)
        total = jnp.where(dc, 0.5 * total, total)
        high = total.astype(BF16)
        low = (total - high.astype(F32)).astype(BF16)
        y = jnp.dot(jnp.concatenate([high, low], axis=0), first_ref[0], preferred_element_type=F32)
        y = y[:16] + y[16:] + jnp.dot(high, first_ref[1], preferred_element_type=F32)
        real = y[0:8, :step] - y[8:16, step:]
        imag = y[0:8, step:] + y[8:16, :step]
        cos, sin = twiddle_ref[0], twiddle_ref[1]
        z = jnp.concatenate([real * cos - imag * sin, real * sin + imag * cos], axis=0)
        series = jnp.dot(last_ref[...], z, precision=lax.Precision.HIGHEST, preferred_element_type=F32)
        for p in range(8):
            out_ref[0, d : d + 1, p * step : (p + 1) * step] = series[p : p + 1, :]


def call(kernel, out_shape, in_specs, scratch=(), vmem=52000, name=None):
    return pl.pallas_call(
        kernel,
        out_shape=out_shape,
        in_specs=in_specs,
        out_specs=jax.tree.map(lambda _: VMEM, out_shape),
        scratch_shapes=list(scratch),
        compiler_params=pltpu.CompilerParams(vmem_limit_bytes=vmem * 2**10),
        name=name,
    )


def body(filterbank, channel_mask, band_edges, dm_delays):
    _, local, samples = filterbank.shape
    group = lax.axis_size("wide")
    channels = local * group
    trials = dm_delays.shape[0]
    lanes = 8 * trials
    bins = samples // 4
    blocks = bins // 64
    shape = jax.ShapeDtypeStruct
    x = filterbank.reshape(local, samples)
    keep = channel_mask.reshape(1, local)
    power_lanes = -(-(band_edges.shape[0] + 1) * NBLK // 128) * 128
    edges_scratch = pltpu.SMEM(band_edges.shape, jnp.int32)
    keep_scratch = pltpu.VMEM(keep.shape, jnp.int32)

    power, info = call(
        functools.partial(power_kernel, group),
        (shape((group, power_lanes), F32), shape((HEAD + 8, max(local, lanes)), F32)),
        [HBM] * 4,
        [
            pltpu.VMEM((local, samples), BF16),
            pltpu.VMEM((2, local, 128), F32),
            edges_scratch,
            keep_scratch,
            pltpu.SMEM(dm_delays.shape, jnp.int32),
            pltpu.SemaphoreType.DMA((3,)),
            pltpu.SemaphoreType.DMA((4,)),
        ],
        vmem=65536,
        name="band_power",
    )(band_edges, keep, dm_delays, x)
    all_power = lax.all_to_all(power, "wide", 0, 0, tiled=True)

    pack, x = call(
        functools.partial(phase_kernel, group),
        (shape((HEAD + 8 * local, lanes), F32), shape((local, samples), BF16)),
        [VMEM, HBM],
        [pltpu.SemaphoreType.DMA],
        name="phases",
    )(info, x)

    table = forward_tables(samples)
    partial = call(
        main_kernel,
        shape((trials, 16, 128), BF16),
        [VMEM] * 3 + [HBM],
        [
            pltpu.VMEM(table.shape, BF16),
            pltpu.VMEM((local, 11 * samples // 8), BF16),
            pltpu.VMEM((4, blocks, 32, local), BF16),
            pltpu.VMEM((2, local, lanes), F32),
            pltpu.VMEM((4, 2, local, lanes), F32),
            pltpu.VMEM((2, blocks, 8, lanes), F32),
            pltpu.SemaphoreType.DMA((8,)),
        ],
        name="dedisperse",
    )(all_power, x, pack, jnp.asarray(table))
    got = lax.all_to_all(partial, "wide", 0, 0, tiled=True)

    first, twiddle, last = inverse_tables(samples, channels)
    return call(
        functools.partial(inverse_kernel, group),
        shape((1, trials // group, samples), F32),
        [VMEM] * 4,
        vmem=8192,
        name="inverse",
    )(got, jnp.asarray(first), jnp.asarray(twiddle), jnp.asarray(last))


def solution(mesh):
    return jax.shard_map(
        body,
        mesh=mesh,
        in_specs=(P("beam", "wide", None), P(("beam", "wide")), P(), P()),
        out_specs=P("beam", "wide", None),
        check_vma=False,
    )
```

```python
import functools
import math

import jax
import jax.numpy as jnp
import ml_dtypes
import numpy as np
from jax import lax
from jax.experimental import pallas as pl
from jax.experimental.pallas import tpu as pltpu
from jax.sharding import PartitionSpec as P

NBLK = 8
HEAD = 3 * NBLK
F32 = jnp.float32
BF16 = jnp.bfloat16
VMEM = pl.BlockSpec(memory_space=pltpu.VMEM)
HBM = pl.BlockSpec(memory_space=pltpu.HBM)


def trig_coefficients(terms):
    n = 400
    y = 0.125 + 0.125 * np.cos(np.pi * (np.arange(n) + 0.5) / n)
    x = np.sqrt(y)
    out = []
    for values in (np.cos(2 * np.pi * x), np.sin(2 * np.pi * x) / x):
        fit = np.polynomial.Chebyshev.fit(y, values, terms - 1, domain=[0.0, 0.25])
        out.append([float(v) for v in fit.convert(kind=np.polynomial.Polynomial).coef])
    return out


def cos_sin_cycles(x):
    cos_c, sin_c = trig_coefficients(9)
    x = x - jnp.round(x)
    y = x * x
    c = jnp.full_like(x, cos_c[-1])
    s = jnp.full_like(x, sin_c[-1])
    for a, b in zip(cos_c[-2::-1], sin_c[-2::-1]):
        c = c * y + a
        s = s * y + b
    return c, s * x


def class_bins(r, bins):
    b = np.arange(bins // 64)[:, None]
    i = (np.arange(8)[None, :] - r) % 8
    return 64 * b + 8 * i + r


def forward_tables(samples):
    bins = samples // 4
    u = np.arange(samples // NBLK)
    tables = []
    for r in range(8):
        f = class_bins(r, bins)[:, :, None]
        angle = 2.0 * np.pi * ((f * u) % samples) / samples
        tables.append(np.stack([np.cos(angle), -np.sin(angle)]).reshape(bins // 4, -1))
    return np.concatenate(tables, 0).astype(ml_dtypes.bfloat16)


def inverse_tables(samples, channels):
    bins = samples // 4
    g = np.arange(bins // 8)[:, None]
    q = np.arange(samples // 8)[None, :]
    angle = 2.0 * np.pi * ((8 * g * q) % samples) / samples
    exact = np.concatenate([np.cos(angle), np.sin(angle)], 1)
    high = exact.astype(ml_dtypes.bfloat16)
    first = np.stack([high, (exact - high.astype(np.float64)).astype(ml_dtypes.bfloat16)])
    r = np.arange(8)[:, None]
    weight = 2.0 / (samples * math.sqrt(channels))
    angle = 2.0 * np.pi * r * q / samples
    twiddle = (weight * np.stack([np.cos(angle), np.sin(angle)])).astype(np.float32)
    p = np.arange(8)[:, None]
    angle = 2.0 * np.pi * ((p * r.T) % 8) / 8
    last = np.concatenate([np.cos(angle), -np.sin(angle)], 1).astype(np.float32)
    return first, twiddle, last


def band_place(edges_ref, first, channels):
    band = jnp.int32(0)
    cut = jnp.int32(channels)
    for e in range(edges_ref.shape[0]):
        edge = edges_ref[e]
        band = band + (edge <= first).astype(jnp.int32)
        cut = jnp.where(edge > first, jnp.minimum(cut, edge), cut)
    return band, cut


def power_kernel(
    group, edges_hbm, keep_hbm, delays_hbm, x_hbm, out_ref, info_ref,
    x_ref, mask_ref, edges_ref, keep_ref, delays_ref, sems, x_sems,
):
    local = x_ref.shape[0]
    window = x_ref.shape[1] // NBLK
    parts = x_sems.shape[0]
    step = local // parts
    channels = local * group
    small = [
        pltpu.make_async_copy(source, target, sems.at[n])
        for n, (source, target) in enumerate(((edges_hbm, edges_ref), (keep_hbm, keep_ref), (delays_hbm, delays_ref)))
    ]
    large = [
        pltpu.make_async_copy(x_hbm.at[pl.ds(n * step, step)], x_ref.at[pl.ds(n * step, step)], x_sems.at[n])
        for n in range(parts)
    ]
    for copy in small + large:
        copy.start()
    for copy in small:
        copy.wait()
    first = lax.axis_index("wide") * local
    band = jnp.int32(0)
    cut = jnp.int32(channels)
    edges = edges_ref.shape[0]
    for e in range(edges):
        edge = edges_ref[e]
        band = band + (edge <= first).astype(jnp.int32)
        cut = jnp.where(edge > first, jnp.minimum(cut, edge), cut)
    ids = first + lax.broadcasted_iota(jnp.int32, (1, local), 1)
    keep = keep_ref[...].astype(F32)
    masks = [jnp.where(inside, keep, 0.0) for inside in (ids < cut, ids >= cut)]
    for j in range(2):
        mask_ref[j] = jnp.broadcast_to(masks[j], (128, local)).T

    wide = info_ref.shape[1]
    lane = lax.broadcasted_iota(jnp.int32, (2 * NBLK, wide), 1)
    row = lax.broadcasted_iota(jnp.int32, (2 * NBLK, wide), 0)
    place = lane == band * NBLK + row
    info_ref[: 2 * NBLK, :] = jnp.where(place, 1.0, 0.0)
    width = jnp.ones((8, wide), F32)
    for j in range(edges + 1):
        low = edges_ref[j - 1] if j else jnp.int32(0)
        high = edges_ref[j] if j < edges else jnp.int32(channels)
        width = jnp.where((lane[:8] >> 3) == j, (high - low).astype(F32), width)
    info_ref[2 * NBLK : HEAD, :] = width
    delay = jnp.zeros((8, wide), F32)
    for d in range(delays_ref.shape[0]):
        delay = jnp.where((lane[:8] >> 3) == d, delays_ref[d].astype(F32), delay)
    info_ref[HEAD:, :] = delay
    for j in range(2):
        info_ref[HEAD + j : HEAD + j + 1, :local] = masks[j]

    totals = [[jnp.zeros((16, 128), F32) for _ in range(NBLK)] for _ in range(2)]
    for n in range(parts):
        large[n].wait()
        for c in range(n * step, (n + 1) * step, 16):
            for k in range(NBLK):
                squares = jnp.zeros((16, 128), F32)
                for u in range(k * window, (k + 1) * window, 128):
                    v = x_ref[c : c + 16, u : u + 128].astype(F32)
                    squares = squares + v * v
                for j in range(2):
                    totals[j][k] = totals[j][k] + squares * mask_ref[j, c : c + 16, :]
    flat = jnp.concatenate([jnp.sum(t, axis=0, keepdims=True) for row in totals for t in row], axis=0)
    sums = jnp.sum(flat, axis=1, keepdims=True) * (1.0 / window)
    lanes = out_ref.shape[1]
    placed = jnp.where(place[:, :lanes], jnp.broadcast_to(sums, (2 * NBLK, lanes)), 0.0)
    out_ref[...] = jnp.broadcast_to(jnp.sum(placed, axis=0, keepdims=True), out_ref.shape)


def turned(a, b):
    return a[0] * b[0] - a[1] * b[1], a[1] * b[0] + a[0] * b[1]


def phase_kernel(group, info_ref, x_hbm, pack_ref, x_ref, sem):
    local, samples = x_ref.shape
    lanes = pack_ref.shape[1]
    channels = local * group
    copy = pltpu.make_async_copy(x_hbm, x_ref, sem)
    copy.start()
    first = lax.axis_index("wide") * local
    pack_ref[:HEAD, :] = info_ref[:HEAD, :lanes]
    for j in range(2):
        mask = jnp.broadcast_to(info_ref[HEAD + j : HEAD + j + 1, :local], (lanes, local))
        pack_ref[HEAD + j * local : HEAD + (j + 1) * local, :] = mask.T
    lane = lax.broadcasted_iota(jnp.int32, (16, lanes), 1)
    delay = jnp.broadcast_to(info_ref[HEAD + 2 : HEAD + 3, :lanes], (16, lanes))
    bins = ((3.5 + 8.0 * (lane & 7).astype(F32)) * delay, 64.0 * delay, 0.5 * delay)

    def rows(n, carry):
        c = pl.multiple_of(n * 16, 16)
        channel = first + c + lax.broadcasted_iota(jnp.int32, (16, lanes), 0)
        ratio = 0.5 + 0.5 * (channel.astype(F32) + 0.5) / channels
        fraction = (1.0 / (ratio * ratio) - 1.0) / 3.0 / samples
        for m in range(3):
            for q, v in enumerate(cos_sin_cycles(bins[m] * fraction)):
                pack_ref[pl.ds(pl.multiple_of(HEAD + (2 + 2 * m + q) * local + c, 8), 16), :] = v
        return carry

    lax.fori_loop(0, local // 16, rows, 0, unroll=2)
    copy.wait()


def window_classes(y):
    half = math.sqrt(0.5)
    e = [y[k] + y[k + 4] for k in range(4)]
    o = [y[k] - y[k + 4] for k in range(4)]
    a, b = e[0] + e[2], e[1] + e[3]
    p, q = half * (o[1] - o[3]), half * (o[1] + o[3])
    return [a + b, a - b, o[0] + p, -(o[2] + q), e[0] - e[2], e[3] - e[1], o[0] - p, o[2] - q]


def main_kernel(
    power_ref, x_ref, pack_ref, table_hbm,
    out_ref, table_ref, z_ref, spec_ref, state_ref, step_ref, part_ref, table_sems,
):
    local, samples = x_ref.shape
    window = samples // NBLK
    lanes = pack_ref.shape[1]
    rows = table_ref.shape[0] // 8
    head = HEAD + 2 * local
    table_copies = [
        pltpu.make_async_copy(
            table_hbm.at[pl.ds(n * rows, rows)], table_ref.at[pl.ds(n * rows, rows)], table_sems.at[n]
        )
        for n in range(8)
    ]
    for copy in table_copies:
        copy.start()
    power = jnp.sum(power_ref[...], axis=0, keepdims=True)
    wide = power.shape[1]
    inverse = 1.0 / jnp.sqrt(power / pack_ref[2 * NBLK : 2 * NBLK + 1, :wide] + 1e-05)
    column = jnp.sum(pack_ref[: 2 * NBLK, :wide] * inverse, axis=1, keepdims=True)
    column = jnp.broadcast_to(column, (2 * NBLK, 128))
    scale = [
        [jnp.broadcast_to(column[j * NBLK + k : j * NBLK + k + 1, :], (16, 128)) for k in range(NBLK)]
        for j in range(2)
    ]

    waiting = []

    def store(next_stores):
        for ref, index, value in waiting:
            ref[index] = value
        waiting[:] = next_stores

    for c in range(0, local, 16):
        at = slice(c, c + 16)
        m0 = pack_ref[HEAD + c : HEAD + c + 16, :128]
        m1 = pack_ref[HEAD + local + c : HEAD + local + c + 16, :128]
        weight = [m0 * scale[0][k] + m1 * scale[1][k] for k in range(NBLK)]
        for u in range(0, window, 128):
            y = [x_ref[at, k * window + u : k * window + u + 128].astype(F32) * weight[k] for k in range(NBLK)]
            classes = window_classes(y)
            classes += [-classes[m] for m in (3, 5, 7)]
            store([
                (z_ref, (at, slice(m * window + u, m * window + u + 128)), z.astype(BF16))
                for m, z in enumerate(classes)
            ])
    store([])

    blocks = rows // 16
    contract = (((1,), (1,)), ((), ()))

    def put(r, real, imag):
        j, at = (r - 4, 0) if r >= 4 else (3 - r, 16)
        both = jnp.concatenate([v.reshape(blocks, 8, local) for v in (real, imag)], axis=1)
        spec_ref[j, :, at : at + 16, :] = both.astype(BF16)

    def across(table, n):
        return lax.dot_general(table, n, contract, preferred_element_type=F32)

    half = rows // 2
    for r in (0, 4):
        table_copies[r].wait()
        at = r // 4 * window
        found = across(table_ref[r * rows : (r + 1) * rows, :], z_ref[:, at : at + window])
        put(r, found[:half], found[half:])
    for r in (1, 2, 3):
        table_copies[r].wait()
        table_copies[8 - r].wait()
        real, imag, minus = (z_ref[:, n * window : (n + 1) * window] for n in (2 * r, 2 * r + 1, 7 + r))
        (cos_a, sin_a), (cos_b, sin_b) = (
            (table_ref[n * rows : n * rows + half, :], table_ref[n * rows + half : (n + 1) * rows, :]) for n in (r, 8 - r)
        )
        left = [jnp.concatenate(pair, axis=1) for pair in ((sin_a, cos_a), (cos_b, sin_b))]
        plus = across(jnp.concatenate(left, axis=0), jnp.concatenate([real, imag], axis=1))
        left = [jnp.concatenate(pair, axis=1) for pair in ((cos_a, sin_a), (sin_b, cos_b))]
        other = across(jnp.concatenate(left, axis=0), jnp.concatenate([real, minus], axis=1))
        put(r, other[:half], plus[:half])
        put(8 - r, plus[half:], other[half:])

    def phase(m, at):
        return pack_ref[head + m * local + at.start : head + m * local + at.stop, :]

    for c in range(0, local, 16):
        at = slice(c, c + 16)
        step = phase(4, at), phase(5, at)
        one = turned(step, step)
        stores = [(state_ref, (q, at, slice(None)), phase(q, at)) for q in range(2)]
        for j in range(4):
            stores += [(step_ref, (j, q, at, slice(None)), step[q].astype(BF16)) for q in range(2)]
            step = turned(step, one)
        store(stores)
    store([])

    sub = lax.broadcasted_iota(jnp.int32, (8, lanes), 0)
    inner = lax.broadcasted_iota(jnp.int32, (8, lanes), 1) & 7
    skew = (sub - inner) & 7

    def dedisperse(b, carry):
        made = []
        for c in range(0, local, 16):
            at = slice(c, c + 16)
            state = cos0, sin0 = state_ref[0, at, :], state_ref[1, at, :]
            products = []
            cos0, sin0 = cos0.astype(BF16), sin0.astype(BF16)
            for j in range(4):
                cos_j, sin_j = step_ref[j, 0, at, :], step_ref[j, 1, at, :]
                cc, ss, sc, cs = cos0 * cos_j, sin0 * sin_j, sin0 * cos_j, cos0 * sin_j
                for pair in ((cc - ss, sc + cs), (cc + ss, sc - cs)):
                    products.append(jnp.concatenate(pair, axis=1))
            made.append(products)
            moved = turned(state, (phase(2, at), phase(3, at)))
            store([(state_ref, (q, at, slice(None)), moved[q]) for q in range(2)])
        store([])
        tiles = [jnp.concatenate([products[n] for products in made], axis=0) for n in range(8)]
        found = [None] * 8
        for j in range(4):
            both = spec_ref[j, b]
            up = jnp.dot(both[:16], tiles[2 * j], preferred_element_type=F32)
            down = jnp.dot(both[16:], tiles[2 * j + 1], preferred_element_type=F32)
            cos_up, sin_up, cos_down, sin_down = up[:, :lanes], up[:, lanes:], down[:, :lanes], down[:, lanes:]
            found[4 + j] = cos_up[:8] - sin_up[8:], sin_up[:8] + cos_up[8:]
            found[3 - j] = cos_down[:8] - sin_down[8:], sin_down[:8] + cos_down[8:]
        real, imag = found[0]
        for r in range(1, 8):
            real = jnp.where(skew == r, found[r][0], real)
            imag = jnp.where(skew == r, found[r][1], imag)
        for bit in (1, 2, 4):
            move = (inner & bit) != 0
            real = jnp.where(move, pltpu.roll(real, 8 - bit, 0), real)
            imag = jnp.where(move, pltpu.roll(imag, 8 - bit, 0), imag)
        part_ref[0, b] = real
        part_ref[1, b] = imag
        return carry

    lax.fori_loop(0, blocks, dedisperse, 0, unroll=8)

    block = lax.broadcasted_iota(jnp.int32, (8, 128), 1) >> 3
    for half in range(lanes // 128):
        done = []
        for part in range(2):
            v = [part_ref[part, b, :, half * 128 : half * 128 + 128] for b in range(16)]
            for bit in (1, 2, 4, 8):
                w = list(v)
                high = (block & bit) != 0
                for b in range(16):
                    if b & bit:
                        w[b] = jnp.where(high, v[b], pltpu.roll(v[b ^ bit], 128 - 8 * bit, 1))
                    else:
                        w[b] = jnp.where(high, pltpu.roll(v[b ^ bit], 8 * bit, 1), v[b])
                v = w
            done.append(v)
        for d in range(16):
            out_ref[half * 16 + d] = jnp.concatenate([done[0][d], done[1][d]], axis=0).astype(BF16)


def inverse_kernel(group, got_ref, first_ref, twiddle_ref, last_ref, out_ref):
    step = first_ref.shape[2] // 2
    trials = out_ref.shape[1]
    row = lax.broadcasted_iota(jnp.int32, (16, 128), 0)
    lane = lax.broadcasted_iota(jnp.int32, (16, 128), 1)
    dc = ((row & 7) == 0) & (lane == 0)
    for d in range(trials):
        total = got_ref[d].astype(F32)
        for n in range(1, group):
            total = total + got_ref[n * trials + d].astype(F32)
        total = jnp.where(dc, 0.5 * total, total)
        high = total.astype(BF16)
        low = (total - high.astype(F32)).astype(BF16)
        y = jnp.dot(jnp.concatenate([high, low], axis=0), first_ref[0], preferred_element_type=F32)
        y = y[:16] + y[16:] + jnp.dot(high, first_ref[1], preferred_element_type=F32)
        real = y[0:8, :step] - y[8:16, step:]
        imag = y[0:8, step:] + y[8:16, :step]
        cos, sin = twiddle_ref[0], twiddle_ref[1]
        z = jnp.concatenate([real * cos - imag * sin, real * sin + imag * cos], axis=0)
        series = jnp.dot(last_ref[...], z, precision=lax.Precision.HIGHEST, preferred_element_type=F32)
        for p in range(8):
            out_ref[0, d : d + 1, p * step : (p + 1) * step] = series[p : p + 1, :]


def call(kernel, out_shape, in_specs, scratch=(), vmem=52000, name=None):
    return pl.pallas_call(
        kernel,
        out_shape=out_shape,
        in_specs=in_specs,
        out_specs=jax.tree.map(lambda _: VMEM, out_shape),
        scratch_shapes=list(scratch),
        compiler_params=pltpu.CompilerParams(vmem_limit_bytes=vmem * 2**10),
        name=name,
    )


def body(filterbank, channel_mask, band_edges, dm_delays):
    _, local, samples = filterbank.shape
    group = lax.axis_size("wide")
    channels = local * group
    trials = dm_delays.shape[0]
    lanes = 8 * trials
    bins = samples // 4
    blocks = bins // 64
    shape = jax.ShapeDtypeStruct
    x = filterbank.reshape(local, samples)
    keep = channel_mask.reshape(1, local)
    power_lanes = -(-(band_edges.shape[0] + 1) * NBLK // 128) * 128
    edges_scratch = pltpu.SMEM(band_edges.shape, jnp.int32)
    keep_scratch = pltpu.VMEM(keep.shape, jnp.int32)

    power, info = call(
        functools.partial(power_kernel, group),
        (shape((group, power_lanes), F32), shape((HEAD + 8, max(local, lanes)), F32)),
        [HBM] * 4,
        [
            pltpu.VMEM((local, samples), BF16),
            pltpu.VMEM((2, local, 128), F32),
            edges_scratch,
            keep_scratch,
            pltpu.SMEM(dm_delays.shape, jnp.int32),
            pltpu.SemaphoreType.DMA((3,)),
            pltpu.SemaphoreType.DMA((4,)),
        ],
        vmem=65536,
        name="band_power",
    )(band_edges, keep, dm_delays, x)
    all_power = lax.all_to_all(power, "wide", 0, 0, tiled=True)

    pack, x = call(
        functools.partial(phase_kernel, group),
        (shape((HEAD + 8 * local, lanes), F32), shape((local, samples), BF16)),
        [VMEM, HBM],
        [pltpu.SemaphoreType.DMA],
        name="phases",
    )(info, x)

    table = forward_tables(samples)
    partial = call(
        main_kernel,
        shape((trials, 16, 128), BF16),
        [VMEM] * 3 + [HBM],
        [
            pltpu.VMEM(table.shape, BF16),
            pltpu.VMEM((local, 11 * samples // 8), BF16),
            pltpu.VMEM((4, blocks, 32, local), BF16),
            pltpu.VMEM((2, local, lanes), F32),
            pltpu.VMEM((4, 2, local, lanes), BF16),
            pltpu.VMEM((2, blocks, 8, lanes), F32),
            pltpu.SemaphoreType.DMA((8,)),
        ],
        name="dedisperse",
    )(all_power, x, pack, jnp.asarray(table))
    got = lax.all_to_all(partial, "wide", 0, 0, tiled=True)

    first, twiddle, last = inverse_tables(samples, channels)
    return call(
        functools.partial(inverse_kernel, group),
        shape((1, trials // group, samples), F32),
        [VMEM] * 4,
        vmem=8192,
        name="inverse",
    )(got, jnp.asarray(first), jnp.asarray(twiddle), jnp.asarray(last))


def solution(mesh):
    return jax.shard_map(
        body,
        mesh=mesh,
        in_specs=(P("beam", "wide", None), P(("beam", "wide")), P(), P()),
        out_specs=P("beam", "wide", None),
        check_vma=False,
    )
```

```python
import functools
import math

import jax
import jax.numpy as jnp
import ml_dtypes
import numpy as np
from jax import lax
from jax.experimental import pallas as pl
from jax.experimental.pallas import tpu as pltpu
from jax.sharding import PartitionSpec as P

NBLK = 8
HEAD = 3 * NBLK
AT_ONCE = 4
F32 = jnp.float32
BF16 = jnp.bfloat16
VMEM = pl.BlockSpec(memory_space=pltpu.VMEM)
HBM = pl.BlockSpec(memory_space=pltpu.HBM)


def trig_coefficients(terms):
    n = 400
    y = 0.125 + 0.125 * np.cos(np.pi * (np.arange(n) + 0.5) / n)
    x = np.sqrt(y)
    out = []
    for values in (np.cos(2 * np.pi * x), np.sin(2 * np.pi * x) / x):
        fit = np.polynomial.Chebyshev.fit(y, values, terms - 1, domain=[0.0, 0.25])
        out.append([float(v) for v in fit.convert(kind=np.polynomial.Polynomial).coef])
    return out


def cos_sin_cycles(x):
    cos_c, sin_c = trig_coefficients(9)
    x = x - jnp.round(x)
    y = x * x
    c = jnp.full_like(x, cos_c[-1])
    s = jnp.full_like(x, sin_c[-1])
    for a, b in zip(cos_c[-2::-1], sin_c[-2::-1]):
        c = c * y + a
        s = s * y + b
    return c, s * x


def class_bins(r, bins):
    b = np.arange(bins // 64)[:, None]
    i = (np.arange(8)[None, :] - r) % 8
    return 64 * b + 8 * i + r


def forward_tables(samples):
    bins = samples // 4
    u = np.arange(samples // NBLK)
    tables = []
    for r in range(8):
        f = class_bins(r, bins)[:, :, None]
        angle = 2.0 * np.pi * ((f * u) % samples) / samples
        tables.append(np.stack([np.cos(angle), -np.sin(angle)]).reshape(bins // 4, -1))
    return np.concatenate(tables, 0).astype(ml_dtypes.bfloat16)


def inverse_tables(samples, channels):
    bins = samples // 4
    g = np.arange(bins // 8)[:, None]
    q = np.arange(samples // 8)[None, :]
    angle = 2.0 * np.pi * ((8 * g * q) % samples) / samples
    exact = np.concatenate([np.cos(angle), np.sin(angle)], 1)
    high = exact.astype(ml_dtypes.bfloat16)
    first = np.stack([high, (exact - high.astype(np.float64)).astype(ml_dtypes.bfloat16)])
    r = np.arange(8)[:, None]
    weight = 2.0 / (samples * math.sqrt(channels))
    angle = 2.0 * np.pi * r * q / samples
    twiddle = (weight * np.stack([np.cos(angle), np.sin(angle)])).astype(np.float32)
    p = np.arange(8)[:, None]
    angle = 2.0 * np.pi * ((p * r.T) % 8) / 8
    last = np.concatenate([np.cos(angle), -np.sin(angle)], 1).astype(np.float32)
    return first, twiddle, last


def band_place(edges_ref, first, channels):
    band = jnp.int32(0)
    cut = jnp.int32(channels)
    for e in range(edges_ref.shape[0]):
        edge = edges_ref[e]
        band = band + (edge <= first).astype(jnp.int32)
        cut = jnp.where(edge > first, jnp.minimum(cut, edge), cut)
    return band, cut


def power_kernel(
    group, edges_hbm, keep_hbm, delays_hbm, x_hbm, out_ref, info_ref,
    x_ref, mask_ref, edges_ref, keep_ref, delays_ref, sems, x_sems,
):
    local = x_ref.shape[0]
    window = x_ref.shape[1] // NBLK
    parts = x_sems.shape[0]
    step = local // parts
    channels = local * group
    small = [
        pltpu.make_async_copy(source, target, sems.at[n])
        for n, (source, target) in enumerate(((edges_hbm, edges_ref), (keep_hbm, keep_ref), (delays_hbm, delays_ref)))
    ]
    large = [
        pltpu.make_async_copy(x_hbm.at[pl.ds(n * step, step)], x_ref.at[pl.ds(n * step, step)], x_sems.at[n])
        for n in range(parts)
    ]
    for copy in small + large:
        copy.start()
    for copy in small:
        copy.wait()
    first = lax.axis_index("wide") * local
    band = jnp.int32(0)
    cut = jnp.int32(channels)
    edges = edges_ref.shape[0]
    for e in range(edges):
        edge = edges_ref[e]
        band = band + (edge <= first).astype(jnp.int32)
        cut = jnp.where(edge > first, jnp.minimum(cut, edge), cut)
    ids = first + lax.broadcasted_iota(jnp.int32, (1, local), 1)
    keep = keep_ref[...].astype(F32)
    masks = [jnp.where(inside, keep, 0.0) for inside in (ids < cut, ids >= cut)]
    for j in range(2):
        mask_ref[j] = jnp.broadcast_to(masks[j], (128, local)).T

    wide = info_ref.shape[1]
    lane = lax.broadcasted_iota(jnp.int32, (2 * NBLK, wide), 1)
    row = lax.broadcasted_iota(jnp.int32, (2 * NBLK, wide), 0)
    place = lane == band * NBLK + row
    info_ref[: 2 * NBLK, :] = jnp.where(place, 1.0, 0.0)
    width = jnp.ones((8, wide), F32)
    for j in range(edges + 1):
        low = edges_ref[j - 1] if j else jnp.int32(0)
        high = edges_ref[j] if j < edges else jnp.int32(channels)
        width = jnp.where((lane[:8] >> 3) == j, (high - low).astype(F32), width)
    info_ref[2 * NBLK : HEAD, :] = width
    delay = jnp.zeros((8, wide), F32)
    for d in range(delays_ref.shape[0]):
        delay = jnp.where((lane[:8] >> 3) == d, delays_ref[d].astype(F32), delay)
    info_ref[HEAD:, :] = delay
    for j in range(2):
        info_ref[HEAD + j : HEAD + j + 1, :local] = masks[j]

    totals = [[jnp.zeros((16, 128), F32) for _ in range(NBLK)] for _ in range(2)]
    for n in range(parts):
        large[n].wait()
        for c in range(n * step, (n + 1) * step, 16):
            for k in range(NBLK):
                squares = jnp.zeros((16, 128), F32)
                for u in range(k * window, (k + 1) * window, 128):
                    v = x_ref[c : c + 16, u : u + 128].astype(F32)
                    squares = squares + v * v
                for j in range(2):
                    totals[j][k] = totals[j][k] + squares * mask_ref[j, c : c + 16, :]
    flat = jnp.concatenate([jnp.sum(t, axis=0, keepdims=True) for row in totals for t in row], axis=0)
    sums = jnp.sum(flat, axis=1, keepdims=True) * (1.0 / window)
    lanes = out_ref.shape[1]
    placed = jnp.where(place[:, :lanes], jnp.broadcast_to(sums, (2 * NBLK, lanes)), 0.0)
    out_ref[...] = jnp.broadcast_to(jnp.sum(placed, axis=0, keepdims=True), out_ref.shape)


def turned(a, b):
    return a[0] * b[0] - a[1] * b[1], a[1] * b[0] + a[0] * b[1]


def phase_kernel(group, info_ref, x_hbm, pack_ref, x_ref, sem):
    local, samples = x_ref.shape
    lanes = pack_ref.shape[1]
    channels = local * group
    copy = pltpu.make_async_copy(x_hbm, x_ref, sem)
    copy.start()
    first = lax.axis_index("wide") * local
    pack_ref[:HEAD, :] = info_ref[:HEAD, :lanes]
    for j in range(2):
        mask = jnp.broadcast_to(info_ref[HEAD + j : HEAD + j + 1, :local], (lanes, local))
        pack_ref[HEAD + j * local : HEAD + (j + 1) * local, :] = mask.T
    lane = lax.broadcasted_iota(jnp.int32, (16, lanes), 1)
    delay = jnp.broadcast_to(info_ref[HEAD + 2 : HEAD + 3, :lanes], (16, lanes))
    bins = ((3.5 + 8.0 * (lane & 7).astype(F32)) * delay, 64.0 * delay, 0.5 * delay)

    def rows(n, carry):
        c = pl.multiple_of(n * 16, 16)
        channel = first + c + lax.broadcasted_iota(jnp.int32, (16, lanes), 0)
        ratio = 0.5 + 0.5 * (channel.astype(F32) + 0.5) / channels
        fraction = (1.0 / (ratio * ratio) - 1.0) / 3.0 / samples
        for m in range(3):
            for q, v in enumerate(cos_sin_cycles(bins[m] * fraction)):
                pack_ref[pl.ds(pl.multiple_of(HEAD + (2 + 2 * m + q) * local + c, 8), 16), :] = v
        return carry

    lax.fori_loop(0, local // 16, rows, 0, unroll=2)
    copy.wait()


def window_classes(y):
    half = math.sqrt(0.5)
    e = [y[k] + y[k + 4] for k in range(4)]
    o = [y[k] - y[k + 4] for k in range(4)]
    a, b = e[0] + e[2], e[1] + e[3]
    p, q = half * (o[1] - o[3]), half * (o[1] + o[3])
    return [a + b, a - b, o[0] + p, -(o[2] + q), e[0] - e[2], e[3] - e[1], o[0] - p, o[2] - q]


def main_kernel(
    power_ref, x_ref, pack_ref, table_hbm,
    out_ref, table_ref, z_ref, spec_ref, state_ref, step_ref, part_ref, table_sems,
):
    local, samples = x_ref.shape
    window = samples // NBLK
    lanes = pack_ref.shape[1]
    rows = table_ref.shape[0] // 8
    head = HEAD + 2 * local
    table_copies = [
        pltpu.make_async_copy(
            table_hbm.at[pl.ds(n * rows, rows)], table_ref.at[pl.ds(n * rows, rows)], table_sems.at[n]
        )
        for n in range(8)
    ]
    for n in (0, 4, 1, 7, 2, 6, 3, 5):
        table_copies[n].start()
    power = jnp.sum(power_ref[...], axis=0, keepdims=True)
    wide = power.shape[1]
    inverse = 1.0 / jnp.sqrt(power / pack_ref[2 * NBLK : 2 * NBLK + 1, :wide] + 1e-05)
    column = jnp.sum(pack_ref[: 2 * NBLK, :wide] * inverse, axis=1, keepdims=True)
    column = jnp.broadcast_to(column, (2 * NBLK, 128))
    scale = [
        [jnp.broadcast_to(column[j * NBLK + k : j * NBLK + k + 1, :], (16, 128)) for k in range(NBLK)]
        for j in range(2)
    ]

    waiting = []

    def store(next_stores):
        for ref, index, value in waiting:
            ref[index] = value
        waiting[:] = next_stores

    for c in range(0, local, 16):
        at = slice(c, c + 16)
        m0 = pack_ref[HEAD + c : HEAD + c + 16, :128]
        m1 = pack_ref[HEAD + local + c : HEAD + local + c + 16, :128]
        weight = [m0 * scale[0][k] + m1 * scale[1][k] for k in range(NBLK)]
        for u in range(0, window, 128):
            y = [x_ref[at, k * window + u : k * window + u + 128].astype(F32) * weight[k] for k in range(NBLK)]
            classes = window_classes(y)
            classes += [-classes[m] for m in (3, 5, 7)]
            store([
                (z_ref, (at, slice(m * window + u, m * window + u + 128)), z.astype(BF16))
                for m, z in enumerate(classes)
            ])
    store([])

    blocks = rows // 16
    contract = (((1,), (1,)), ((), ()))

    def put(r, real, imag):
        j, at = (r - 4, 0) if r >= 4 else (3 - r, 16)
        both = jnp.concatenate([v.reshape(blocks, 8, local) for v in (real, imag)], axis=1)
        spec_ref[j, :, at : at + 16, :] = both.astype(BF16)

    def across(table, n):
        return lax.dot_general(table, n, contract, preferred_element_type=F32)

    half = rows // 2
    for r in (0, 4):
        table_copies[r].wait()
        at = r // 4 * window
        found = across(table_ref[r * rows : (r + 1) * rows, :], z_ref[:, at : at + window])
        put(r, found[:half], found[half:])
    for r in (1, 2, 3):
        table_copies[r].wait()
        table_copies[8 - r].wait()
        real, imag, minus = (z_ref[:, n * window : (n + 1) * window] for n in (2 * r, 2 * r + 1, 7 + r))
        (cos_a, sin_a), (cos_b, sin_b) = (
            (table_ref[n * rows : n * rows + half, :], table_ref[n * rows + half : (n + 1) * rows, :]) for n in (r, 8 - r)
        )
        left = [jnp.concatenate(pair, axis=1) for pair in ((sin_a, cos_a), (cos_b, sin_b))]
        plus = across(jnp.concatenate(left, axis=0), jnp.concatenate([real, imag], axis=1))
        left = [jnp.concatenate(pair, axis=1) for pair in ((cos_a, sin_a), (sin_b, cos_b))]
        other = across(jnp.concatenate(left, axis=0), jnp.concatenate([real, minus], axis=1))
        put(r, other[:half], plus[:half])
        put(8 - r, plus[half:], other[half:])

    def phase(m, at):
        return pack_ref[head + m * local + at.start : head + m * local + at.stop, :]

    for c in range(0, local, 16):
        at = slice(c, c + 16)
        step = phase(4, at), phase(5, at)
        one = turned(step, step)
        stores = [(state_ref, (q, at, slice(None)), phase(q, at)) for q in range(2)]
        for j in range(4):
            stores += [(step_ref, (j, q, at, slice(None)), step[q].astype(BF16)) for q in range(2)]
            step = turned(step, one)
        store(stores)
    store([])

    sub = lax.broadcasted_iota(jnp.int32, (8, lanes), 0)
    inner = lax.broadcasted_iota(jnp.int32, (8, lanes), 1) & 7
    skew = (sub - inner) & 7

    def generate(count):
        made = []
        for c in range(0, local, 16):
            at = slice(c, c + 16)
            state = state_ref[0, at, :], state_ref[1, at, :]
            turn = phase(2, at), phase(3, at)
            steps = [(step_ref[j, 0, at, :], step_ref[j, 1, at, :]) for j in range(4)]
            products = []
            for _ in range(count):
                cos0, sin0 = (v.astype(BF16) for v in state)
                for cos_j, sin_j in steps:
                    cc, ss, sc, cs = cos0 * cos_j, sin0 * sin_j, sin0 * cos_j, cos0 * sin_j
                    for pair in ((cc - ss, sc + cs), (cc + ss, sc - cs)):
                        products.append(jnp.concatenate(pair, axis=1))
                state = turned(state, turn)
            made.append(products)
            store([(state_ref, (q, at, slice(None)), state[q]) for q in range(2)])
        store([])
        return [
            [jnp.concatenate([products[8 * n + m] for products in made], axis=0) for m in range(8)] for n in range(count)
        ]

    def dedisperse(b, tiles):
        found = [None] * 8
        for j in range(4):
            both = spec_ref[j, b]
            up = jnp.dot(both[:16], tiles[2 * j], preferred_element_type=F32)
            down = jnp.dot(both[16:], tiles[2 * j + 1], preferred_element_type=F32)
            cos_up, sin_up, cos_down, sin_down = up[:, :lanes], up[:, lanes:], down[:, :lanes], down[:, lanes:]
            found[4 + j] = cos_up[:8] - sin_up[8:], sin_up[:8] + cos_up[8:]
            found[3 - j] = cos_down[:8] - sin_down[8:], sin_down[:8] + cos_down[8:]
        real, imag = found[0]
        for r in range(1, 8):
            real = jnp.where(skew == r, found[r][0], real)
            imag = jnp.where(skew == r, found[r][1], imag)
        for bit in (1, 2, 4):
            move = (inner & bit) != 0
            real = jnp.where(move, pltpu.roll(real, 8 - bit, 0), real)
            imag = jnp.where(move, pltpu.roll(imag, 8 - bit, 0), imag)
        part_ref[0, b] = real
        part_ref[1, b] = imag

    def several(n, carry):
        for m, tiles in enumerate(generate(AT_ONCE)):
            dedisperse(n * AT_ONCE + m, tiles)
        return carry

    lax.fori_loop(0, blocks // AT_ONCE, several, 0, unroll=4)

    block = lax.broadcasted_iota(jnp.int32, (8, 128), 1) >> 3
    for half in range(lanes // 128):
        done = []
        for part in range(2):
            v = [part_ref[part, b, :, half * 128 : half * 128 + 128] for b in range(16)]
            for bit in (1, 2, 4, 8):
                w = list(v)
                high = (block & bit) != 0
                for b in range(16):
                    if b & bit:
                        w[b] = jnp.where(high, v[b], pltpu.roll(v[b ^ bit], 128 - 8 * bit, 1))
                    else:
                        w[b] = jnp.where(high, pltpu.roll(v[b ^ bit], 8 * bit, 1), v[b])
                v = w
            done.append(v)
        for d in range(16):
            out_ref[half * 16 + d] = jnp.concatenate([done[0][d], done[1][d]], axis=0).astype(BF16)


def inverse_kernel(group, got_ref, first_ref, twiddle_ref, last_ref, out_ref):
    step = first_ref.shape[2] // 2
    trials = out_ref.shape[1]
    row = lax.broadcasted_iota(jnp.int32, (16, 128), 0)
    lane = lax.broadcasted_iota(jnp.int32, (16, 128), 1)
    dc = ((row & 7) == 0) & (lane == 0)
    for d in range(trials):
        total = got_ref[d].astype(F32)
        for n in range(1, group):
            total = total + got_ref[n * trials + d].astype(F32)
        total = jnp.where(dc, 0.5 * total, total)
        high = total.astype(BF16)
        low = (total - high.astype(F32)).astype(BF16)
        y = jnp.dot(jnp.concatenate([high, low], axis=0), first_ref[0], preferred_element_type=F32)
        y = y[:16] + y[16:] + jnp.dot(high, first_ref[1], preferred_element_type=F32)
        real = y[0:8, :step] - y[8:16, step:]
        imag = y[0:8, step:] + y[8:16, :step]
        cos, sin = twiddle_ref[0], twiddle_ref[1]
        z = jnp.concatenate([real * cos - imag * sin, real * sin + imag * cos], axis=0)
        series = jnp.dot(last_ref[...], z, precision=lax.Precision.HIGHEST, preferred_element_type=F32)
        for p in range(8):
            out_ref[0, d : d + 1, p * step : (p + 1) * step] = series[p : p + 1, :]


def call(kernel, out_shape, in_specs, scratch=(), vmem=52000, name=None):
    return pl.pallas_call(
        kernel,
        out_shape=out_shape,
        in_specs=in_specs,
        out_specs=jax.tree.map(lambda _: VMEM, out_shape),
        scratch_shapes=list(scratch),
        compiler_params=pltpu.CompilerParams(vmem_limit_bytes=vmem * 2**10),
        name=name,
    )


def body(filterbank, channel_mask, band_edges, dm_delays):
    _, local, samples = filterbank.shape
    group = lax.axis_size("wide")
    channels = local * group
    trials = dm_delays.shape[0]
    lanes = 8 * trials
    bins = samples // 4
    blocks = bins // 64
    shape = jax.ShapeDtypeStruct
    x = filterbank.reshape(local, samples)
    keep = channel_mask.reshape(1, local)
    power_lanes = -(-(band_edges.shape[0] + 1) * NBLK // 128) * 128
    edges_scratch = pltpu.SMEM(band_edges.shape, jnp.int32)
    keep_scratch = pltpu.VMEM(keep.shape, jnp.int32)

    power, info = call(
        functools.partial(power_kernel, group),
        (shape((group, power_lanes), F32), shape((HEAD + 8, max(local, lanes)), F32)),
        [HBM] * 4,
        [
            pltpu.VMEM((local, samples), BF16),
            pltpu.VMEM((2, local, 128), F32),
            edges_scratch,
            keep_scratch,
            pltpu.SMEM(dm_delays.shape, jnp.int32),
            pltpu.SemaphoreType.DMA((3,)),
            pltpu.SemaphoreType.DMA((4,)),
        ],
        vmem=65536,
        name="band_power",
    )(band_edges, keep, dm_delays, x)
    all_power = lax.all_to_all(power, "wide", 0, 0, tiled=True)

    pack, x = call(
        functools.partial(phase_kernel, group),
        (shape((HEAD + 8 * local, lanes), F32), shape((local, samples), BF16)),
        [VMEM, HBM],
        [pltpu.SemaphoreType.DMA],
        name="phases",
    )(info, x)

    table = forward_tables(samples)
    partial = call(
        main_kernel,
        shape((trials, 16, 128), BF16),
        [VMEM] * 3 + [HBM],
        [
            pltpu.VMEM(table.shape, BF16),
            pltpu.VMEM((local, 11 * samples // 8), BF16),
            pltpu.VMEM((4, blocks, 32, local), BF16),
            pltpu.VMEM((2, local, lanes), F32),
            pltpu.VMEM((4, 2, local, lanes), BF16),
            pltpu.VMEM((2, blocks, 8, lanes), F32),
            pltpu.SemaphoreType.DMA((8,)),
        ],
        name="dedisperse",
    )(all_power, x, pack, jnp.asarray(table))
    got = lax.all_to_all(partial, "wide", 0, 0, tiled=True)

    first, twiddle, last = inverse_tables(samples, channels)
    return call(
        functools.partial(inverse_kernel, group),
        shape((1, trials // group, samples), F32),
        [VMEM] * 4,
        vmem=8192,
        name="inverse",
    )(got, jnp.asarray(first), jnp.asarray(twiddle), jnp.asarray(last))


def solution(mesh):
    return jax.shard_map(
        body,
        mesh=mesh,
        in_specs=(P("beam", "wide", None), P(("beam", "wide")), P(), P()),
        out_specs=P("beam", "wide", None),
        check_vma=False,
    )
```

```python
import functools
import math

import jax
import jax.numpy as jnp
import ml_dtypes
import numpy as np
from jax import lax
from jax.experimental import pallas as pl
from jax.experimental.pallas import tpu as pltpu
from jax.sharding import PartitionSpec as P

NBLK = 8
HEAD = 3 * NBLK
F32 = jnp.float32
BF16 = jnp.bfloat16
VMEM = pl.BlockSpec(memory_space=pltpu.VMEM)
HBM = pl.BlockSpec(memory_space=pltpu.HBM)


def trig_coefficients(terms):
    n = 400
    y = 0.125 + 0.125 * np.cos(np.pi * (np.arange(n) + 0.5) / n)
    x = np.sqrt(y)
    out = []
    for values in (np.cos(2 * np.pi * x), np.sin(2 * np.pi * x) / x):
        fit = np.polynomial.Chebyshev.fit(y, values, terms - 1, domain=[0.0, 0.25])
        out.append([float(v) for v in fit.convert(kind=np.polynomial.Polynomial).coef])
    return out


def cos_sin_cycles(x):
    cos_c, sin_c = trig_coefficients(9)
    x = x - jnp.round(x)
    y = x * x
    c = jnp.full_like(x, cos_c[-1])
    s = jnp.full_like(x, sin_c[-1])
    for a, b in zip(cos_c[-2::-1], sin_c[-2::-1]):
        c = c * y + a
        s = s * y + b
    return c, s * x


def class_bins(r, bins):
    b = np.arange(bins // 64)[:, None]
    i = (np.arange(8)[None, :] - r) % 8
    return 64 * b + 8 * i + r


def forward_tables(samples):
    bins = samples // 4
    u = np.arange(samples // NBLK)
    tables = []
    for r in range(8):
        f = class_bins(r, bins)[:, :, None]
        angle = 2.0 * np.pi * ((f * u) % samples) / samples
        tables.append(np.stack([np.cos(angle), -np.sin(angle)]).reshape(bins // 4, -1))
    return np.concatenate(tables, 0).astype(ml_dtypes.bfloat16)


def inverse_tables(samples, channels):
    bins = samples // 4
    g = np.arange(bins // 8)[:, None]
    q = np.arange(samples // 8)[None, :]
    angle = 2.0 * np.pi * ((8 * g * q) % samples) / samples
    exact = np.concatenate([np.cos(angle), np.sin(angle)], 1)
    high = exact.astype(ml_dtypes.bfloat16)
    first = np.stack([high, (exact - high.astype(np.float64)).astype(ml_dtypes.bfloat16)])
    r = np.arange(8)[:, None]
    weight = 2.0 / (samples * math.sqrt(channels))
    angle = 2.0 * np.pi * r * q / samples
    twiddle = (weight * np.stack([np.cos(angle), np.sin(angle)])).astype(np.float32)
    p = np.arange(8)[:, None]
    angle = 2.0 * np.pi * ((p * r.T) % 8) / 8
    exact = np.concatenate([np.cos(angle), -np.sin(angle)], 1)
    high = exact.astype(ml_dtypes.bfloat16)
    last = np.concatenate([high, high, (exact - high.astype(np.float64)).astype(ml_dtypes.bfloat16)], 1)
    return first, twiddle, last


def band_place(edges_ref, first, channels):
    band = jnp.int32(0)
    cut = jnp.int32(channels)
    for e in range(edges_ref.shape[0]):
        edge = edges_ref[e]
        band = band + (edge <= first).astype(jnp.int32)
        cut = jnp.where(edge > first, jnp.minimum(cut, edge), cut)
    return band, cut


def power_kernel(
    group, edges_hbm, keep_hbm, delays_hbm, x_hbm, out_ref, info_ref,
    x_ref, mask_ref, edges_ref, keep_ref, delays_ref, sems, x_sems,
):
    local = x_ref.shape[0]
    window = x_ref.shape[1] // NBLK
    parts = x_sems.shape[0]
    step = local // parts
    channels = local * group
    small = [
        pltpu.make_async_copy(source, target, sems.at[n])
        for n, (source, target) in enumerate(((edges_hbm, edges_ref), (keep_hbm, keep_ref), (delays_hbm, delays_ref)))
    ]
    large = [
        pltpu.make_async_copy(x_hbm.at[pl.ds(n * step, step)], x_ref.at[pl.ds(n * step, step)], x_sems.at[n])
        for n in range(parts)
    ]
    for copy in small + large:
        copy.start()
    for copy in small:
        copy.wait()
    first = lax.axis_index("wide") * local
    band = jnp.int32(0)
    cut = jnp.int32(channels)
    edges = edges_ref.shape[0]
    for e in range(edges):
        edge = edges_ref[e]
        band = band + (edge <= first).astype(jnp.int32)
        cut = jnp.where(edge > first, jnp.minimum(cut, edge), cut)
    ids = first + lax.broadcasted_iota(jnp.int32, (1, local), 1)
    keep = keep_ref[...].astype(F32)
    masks = [jnp.where(inside, keep, 0.0) for inside in (ids < cut, ids >= cut)]
    for j in range(2):
        mask_ref[j] = jnp.broadcast_to(masks[j], (128, local)).T

    wide = info_ref.shape[1]
    lane = lax.broadcasted_iota(jnp.int32, (2 * NBLK, wide), 1)
    row = lax.broadcasted_iota(jnp.int32, (2 * NBLK, wide), 0)
    place = lane == band * NBLK + row
    info_ref[: 2 * NBLK, :] = jnp.where(place, 1.0, 0.0)
    width = jnp.ones((8, wide), F32)
    for j in range(edges + 1):
        low = edges_ref[j - 1] if j else jnp.int32(0)
        high = edges_ref[j] if j < edges else jnp.int32(channels)
        width = jnp.where((lane[:8] >> 3) == j, (high - low).astype(F32), width)
    info_ref[2 * NBLK : HEAD, :] = width
    delay = jnp.zeros((8, wide), F32)
    for d in range(delays_ref.shape[0]):
        delay = jnp.where((lane[:8] >> 3) == d, delays_ref[d].astype(F32), delay)
    info_ref[HEAD:, :] = delay
    for j in range(2):
        info_ref[HEAD + j : HEAD + j + 1, :local] = masks[j]

    totals = [[jnp.zeros((16, 128), F32) for _ in range(NBLK)] for _ in range(2)]
    for n in range(parts):
        large[n].wait()
        for c in range(n * step, (n + 1) * step, 16):
            for k in range(NBLK):
                squares = jnp.zeros((16, 128), F32)
                for u in range(k * window, (k + 1) * window, 128):
                    v = x_ref[c : c + 16, u : u + 128].astype(F32)
                    squares = squares + v * v
                for j in range(2):
                    totals[j][k] = totals[j][k] + squares * mask_ref[j, c : c + 16, :]
    flat = jnp.concatenate([jnp.sum(t, axis=0, keepdims=True) for row in totals for t in row], axis=0)
    sums = jnp.sum(flat, axis=1, keepdims=True) * (1.0 / window)
    lanes = out_ref.shape[1]
    placed = jnp.where(place[:, :lanes], jnp.broadcast_to(sums, (2 * NBLK, lanes)), 0.0)
    out_ref[...] = jnp.broadcast_to(jnp.sum(placed, axis=0, keepdims=True), out_ref.shape)


def turned(a, b):
    return a[0] * b[0] - a[1] * b[1], a[1] * b[0] + a[0] * b[1]


def phase_kernel(group, info_ref, x_hbm, pack_ref, x_ref, sem):
    local, samples = x_ref.shape
    lanes = pack_ref.shape[1]
    channels = local * group
    copy = pltpu.make_async_copy(x_hbm, x_ref, sem)
    copy.start()
    first = lax.axis_index("wide") * local
    pack_ref[:HEAD, :] = info_ref[:HEAD, :lanes]
    for j in range(2):
        mask = jnp.broadcast_to(info_ref[HEAD + j : HEAD + j + 1, :local], (lanes, local))
        pack_ref[HEAD + j * local : HEAD + (j + 1) * local, :] = mask.T
    lane = lax.broadcasted_iota(jnp.int32, (16, lanes), 1)
    delay = jnp.broadcast_to(info_ref[HEAD + 2 : HEAD + 3, :lanes], (16, lanes))
    bins = ((3.5 + 8.0 * (lane & 7).astype(F32)) * delay, 64.0 * delay, 0.5 * delay)

    def rows(n, carry):
        c = pl.multiple_of(n * 16, 16)
        channel = first + c + lax.broadcasted_iota(jnp.int32, (16, lanes), 0)
        ratio = 0.5 + 0.5 * (channel.astype(F32) + 0.5) / channels
        fraction = (1.0 / (ratio * ratio) - 1.0) / 3.0 / samples
        for m in range(3):
            for q, v in enumerate(cos_sin_cycles(bins[m] * fraction)):
                pack_ref[pl.ds(pl.multiple_of(HEAD + (2 + 2 * m + q) * local + c, 8), 16), :] = v
        return carry

    lax.fori_loop(0, local // 16, rows, 0, unroll=2)
    copy.wait()


def window_classes(y):
    half = math.sqrt(0.5)
    e = [y[k] + y[k + 4] for k in range(4)]
    o = [y[k] - y[k + 4] for k in range(4)]
    a, b = e[0] + e[2], e[1] + e[3]
    p, q = half * (o[1] - o[3]), half * (o[1] + o[3])
    return [a + b, a - b, o[0] + p, -(o[2] + q), e[0] - e[2], e[3] - e[1], o[0] - p, o[2] - q]


def main_kernel(
    power_ref, x_ref, pack_ref, table_hbm,
    out_ref, table_ref, z_ref, spec_ref, state_ref, step_ref, part_ref, table_sems,
):
    local, samples = x_ref.shape
    window = samples // NBLK
    lanes = pack_ref.shape[1]
    rows = table_ref.shape[0] // 8
    head = HEAD + 2 * local
    table_copies = [
        pltpu.make_async_copy(
            table_hbm.at[pl.ds(n * rows, rows)], table_ref.at[pl.ds(n * rows, rows)], table_sems.at[n]
        )
        for n in range(8)
    ]
    for copy in table_copies:
        copy.start()
    power = jnp.sum(power_ref[...], axis=0, keepdims=True)
    wide = power.shape[1]
    inverse = 1.0 / jnp.sqrt(power / pack_ref[2 * NBLK : 2 * NBLK + 1, :wide] + 1e-05)
    column = jnp.sum(pack_ref[: 2 * NBLK, :wide] * inverse, axis=1, keepdims=True)
    column = jnp.broadcast_to(column, (2 * NBLK, 128))
    scale = [
        [jnp.broadcast_to(column[j * NBLK + k : j * NBLK + k + 1, :], (16, 128)) for k in range(NBLK)]
        for j in range(2)
    ]

    waiting = []

    def store(next_stores):
        for ref, index, value in waiting:
            ref[index] = value
        waiting[:] = next_stores

    for c in range(0, local, 16):
        at = slice(c, c + 16)
        m0 = pack_ref[HEAD + c : HEAD + c + 16, :128]
        m1 = pack_ref[HEAD + local + c : HEAD + local + c + 16, :128]
        weight = [m0 * scale[0][k] + m1 * scale[1][k] for k in range(NBLK)]
        for u in range(0, window, 128):
            y = [x_ref[at, k * window + u : k * window + u + 128].astype(F32) * weight[k] for k in range(NBLK)]
            classes = window_classes(y)
            classes += [-classes[m] for m in (3, 5, 7)]
            store([
                (z_ref, (at, slice(m * window + u, m * window + u + 128)), z.astype(BF16))
                for m, z in enumerate(classes)
            ])
    store([])

    blocks = rows // 16
    contract = (((1,), (1,)), ((), ()))

    def put(r, real, imag):
        j, at = (r - 4, 0) if r >= 4 else (3 - r, 16)
        both = jnp.concatenate([v.reshape(blocks, 8, local) for v in (real, imag)], axis=1)
        spec_ref[j, :, at : at + 16, :] = both.astype(BF16)

    def across(table, n):
        return lax.dot_general(table, n, contract, preferred_element_type=F32)

    half = rows // 2
    for r in (0, 4):
        table_copies[r].wait()
        at = r // 4 * window
        found = across(table_ref[r * rows : (r + 1) * rows, :], z_ref[:, at : at + window])
        put(r, found[:half], found[half:])
    for r in (1, 2, 3):
        table_copies[r].wait()
        table_copies[8 - r].wait()
        real, imag, minus = (z_ref[:, n * window : (n + 1) * window] for n in (2 * r, 2 * r + 1, 7 + r))
        (cos_a, sin_a), (cos_b, sin_b) = (
            (table_ref[n * rows : n * rows + half, :], table_ref[n * rows + half : (n + 1) * rows, :]) for n in (r, 8 - r)
        )
        left = [jnp.concatenate(pair, axis=1) for pair in ((sin_a, cos_a), (cos_b, sin_b))]
        plus = across(jnp.concatenate(left, axis=0), jnp.concatenate([real, imag], axis=1))
        left = [jnp.concatenate(pair, axis=1) for pair in ((cos_a, sin_a), (sin_b, cos_b))]
        other = across(jnp.concatenate(left, axis=0), jnp.concatenate([real, minus], axis=1))
        put(r, other[:half], plus[:half])
        put(8 - r, plus[half:], other[half:])

    def phase(m, at):
        return pack_ref[head + m * local + at.start : head + m * local + at.stop, :]

    for c in range(0, local, 16):
        at = slice(c, c + 16)
        step = phase(4, at), phase(5, at)
        one = turned(step, step)
        stores = [(state_ref, (q, at, slice(None)), phase(q, at)) for q in range(2)]
        for j in range(4):
            stores += [(step_ref, (j, q, at, slice(None)), step[q].astype(BF16)) for q in range(2)]
            step = turned(step, one)
        store(stores)
    store([])

    sub = lax.broadcasted_iota(jnp.int32, (8, lanes), 0)
    inner = lax.broadcasted_iota(jnp.int32, (8, lanes), 1) & 7
    skew = (sub - inner) & 7

    def dedisperse(b, carry):
        made = []
        for c in range(0, local, 16):
            at = slice(c, c + 16)
            state = cos0, sin0 = state_ref[0, at, :], state_ref[1, at, :]
            products = []
            cos0, sin0 = cos0.astype(BF16), sin0.astype(BF16)
            for j in range(4):
                cos_j, sin_j = step_ref[j, 0, at, :], step_ref[j, 1, at, :]
                cc, ss, sc, cs = cos0 * cos_j, sin0 * sin_j, sin0 * cos_j, cos0 * sin_j
                for pair in ((cc - ss, sc + cs), (cc + ss, sc - cs)):
                    products.append(jnp.concatenate(pair, axis=1))
            made.append(products)
            moved = turned(state, (phase(2, at), phase(3, at)))
            store([(state_ref, (q, at, slice(None)), moved[q]) for q in range(2)])
        store([])
        tiles = [jnp.concatenate([products[n] for products in made], axis=0) for n in range(8)]
        found = [None] * 8
        for j in range(4):
            both = spec_ref[j, b]
            up = jnp.dot(both[:16], tiles[2 * j], preferred_element_type=F32)
            down = jnp.dot(both[16:], tiles[2 * j + 1], preferred_element_type=F32)
            cos_up, sin_up, cos_down, sin_down = up[:, :lanes], up[:, lanes:], down[:, :lanes], down[:, lanes:]
            found[4 + j] = cos_up[:8] - sin_up[8:], sin_up[:8] + cos_up[8:]
            found[3 - j] = cos_down[:8] - sin_down[8:], sin_down[:8] + cos_down[8:]
        real, imag = found[0]
        for r in range(1, 8):
            real = jnp.where(skew == r, found[r][0], real)
            imag = jnp.where(skew == r, found[r][1], imag)
        for bit in (1, 2, 4):
            move = (inner & bit) != 0
            real = jnp.where(move, pltpu.roll(real, 8 - bit, 0), real)
            imag = jnp.where(move, pltpu.roll(imag, 8 - bit, 0), imag)
        part_ref[0, b] = real
        part_ref[1, b] = imag
        return carry

    lax.fori_loop(0, blocks, dedisperse, 0, unroll=8)

    block = lax.broadcasted_iota(jnp.int32, (8, 128), 1) >> 3
    for half in range(lanes // 128):
        done = []
        for part in range(2):
            v = [part_ref[part, b, :, half * 128 : half * 128 + 128] for b in range(16)]
            for bit in (1, 2, 4, 8):
                w = list(v)
                high = (block & bit) != 0
                for b in range(16):
                    if b & bit:
                        w[b] = jnp.where(high, v[b], pltpu.roll(v[b ^ bit], 128 - 8 * bit, 1))
                    else:
                        w[b] = jnp.where(high, pltpu.roll(v[b ^ bit], 8 * bit, 1), v[b])
                v = w
            done.append(v)
        for d in range(16):
            out_ref[half * 16 + d] = jnp.concatenate([done[0][d], done[1][d]], axis=0).astype(BF16)


def inverse_kernel(group, got_ref, first_ref, twiddle_ref, last_ref, out_ref):
    step = first_ref.shape[2] // 2
    trials = out_ref.shape[1]
    row = lax.broadcasted_iota(jnp.int32, (16, 128), 0)
    lane = lax.broadcasted_iota(jnp.int32, (16, 128), 1)
    dc = ((row & 7) == 0) & (lane == 0)
    for d in range(trials):
        total = got_ref[d].astype(F32)
        for n in range(1, group):
            total = total + got_ref[n * trials + d].astype(F32)
        total = jnp.where(dc, 0.5 * total, total)
        high = total.astype(BF16)
        low = (total - high.astype(F32)).astype(BF16)
        y = jnp.dot(jnp.concatenate([high, low], axis=0), first_ref[0], preferred_element_type=F32)
        y = y[:16] + y[16:] + jnp.dot(high, first_ref[1], preferred_element_type=F32)
        real = y[0:8, :step] - y[8:16, step:]
        imag = y[0:8, step:] + y[8:16, :step]
        cos, sin = twiddle_ref[0], twiddle_ref[1]
        z = jnp.concatenate([real * cos - imag * sin, real * sin + imag * cos], axis=0)
        high = z.astype(BF16)
        low = (z - high.astype(F32)).astype(BF16)
        series = jnp.dot(last_ref[...], jnp.concatenate([high, low, high], axis=0), preferred_element_type=F32)
        for p in range(8):
            out_ref[0, d : d + 1, p * step : (p + 1) * step] = series[p : p + 1, :]


def call(kernel, out_shape, in_specs, scratch=(), vmem=52000, name=None):
    return pl.pallas_call(
        kernel,
        out_shape=out_shape,
        in_specs=in_specs,
        out_specs=jax.tree.map(lambda _: VMEM, out_shape),
        scratch_shapes=list(scratch),
        compiler_params=pltpu.CompilerParams(vmem_limit_bytes=vmem * 2**10),
        name=name,
    )


def body(filterbank, channel_mask, band_edges, dm_delays):
    _, local, samples = filterbank.shape
    group = lax.axis_size("wide")
    channels = local * group
    trials = dm_delays.shape[0]
    lanes = 8 * trials
    bins = samples // 4
    blocks = bins // 64
    shape = jax.ShapeDtypeStruct
    x = filterbank.reshape(local, samples)
    keep = channel_mask.reshape(1, local)
    power_lanes = -(-(band_edges.shape[0] + 1) * NBLK // 128) * 128
    edges_scratch = pltpu.SMEM(band_edges.shape, jnp.int32)
    keep_scratch = pltpu.VMEM(keep.shape, jnp.int32)

    power, info = call(
        functools.partial(power_kernel, group),
        (shape((group, power_lanes), F32), shape((HEAD + 8, max(local, lanes)), F32)),
        [HBM] * 4,
        [
            pltpu.VMEM((local, samples), BF16),
            pltpu.VMEM((2, local, 128), F32),
            edges_scratch,
            keep_scratch,
            pltpu.SMEM(dm_delays.shape, jnp.int32),
            pltpu.SemaphoreType.DMA((3,)),
            pltpu.SemaphoreType.DMA((4,)),
        ],
        vmem=65536,
        name="band_power",
    )(band_edges, keep, dm_delays, x)
    all_power = lax.all_to_all(power, "wide", 0, 0, tiled=True)

    pack, x = call(
        functools.partial(phase_kernel, group),
        (shape((HEAD + 8 * local, lanes), F32), shape((local, samples), BF16)),
        [VMEM, HBM],
        [pltpu.SemaphoreType.DMA],
        name="phases",
    )(info, x)

    table = forward_tables(samples)
    partial = call(
        main_kernel,
        shape((trials, 16, 128), BF16),
        [VMEM] * 3 + [HBM],
        [
            pltpu.VMEM(table.shape, BF16),
            pltpu.VMEM((local, 11 * samples // 8), BF16),
            pltpu.VMEM((4, blocks, 32, local), BF16),
            pltpu.VMEM((2, local, lanes), F32),
            pltpu.VMEM((4, 2, local, lanes), BF16),
            pltpu.VMEM((2, blocks, 8, lanes), F32),
            pltpu.SemaphoreType.DMA((8,)),
        ],
        name="dedisperse",
    )(all_power, x, pack, jnp.asarray(table))
    got = lax.all_to_all(partial, "wide", 0, 0, tiled=True)

    first, twiddle, last = inverse_tables(samples, channels)
    return call(
        functools.partial(inverse_kernel, group),
        shape((1, trials // group, samples), F32),
        [VMEM] * 4,
        vmem=8192,
        name="inverse",
    )(got, jnp.asarray(first), jnp.asarray(twiddle), jnp.asarray(last))


def solution(mesh):
    return jax.shard_map(
        body,
        mesh=mesh,
        in_specs=(P("beam", "wide", None), P(("beam", "wide")), P(), P()),
        out_specs=P("beam", "wide", None),
        check_vma=False,
    )
```

```python
import functools
import math

import jax
import jax.numpy as jnp
import ml_dtypes
import numpy as np
from jax import lax
from jax.experimental import pallas as pl
from jax.experimental.pallas import tpu as pltpu
from jax.sharding import PartitionSpec as P

NBLK = 8
HEAD = 3 * NBLK
AT_ONCE = 2
F32 = jnp.float32
BF16 = jnp.bfloat16
VMEM = pl.BlockSpec(memory_space=pltpu.VMEM)
HBM = pl.BlockSpec(memory_space=pltpu.HBM)


def trig_coefficients(terms):
    n = 400
    y = 0.125 + 0.125 * np.cos(np.pi * (np.arange(n) + 0.5) / n)
    x = np.sqrt(y)
    out = []
    for values in (np.cos(2 * np.pi * x), np.sin(2 * np.pi * x) / x):
        fit = np.polynomial.Chebyshev.fit(y, values, terms - 1, domain=[0.0, 0.25])
        out.append([float(v) for v in fit.convert(kind=np.polynomial.Polynomial).coef])
    return out


def cos_sin_cycles(x):
    cos_c, sin_c = trig_coefficients(9)
    x = x - jnp.round(x)
    y = x * x
    c = jnp.full_like(x, cos_c[-1])
    s = jnp.full_like(x, sin_c[-1])
    for a, b in zip(cos_c[-2::-1], sin_c[-2::-1]):
        c = c * y + a
        s = s * y + b
    return c, s * x


def class_bins(r, bins):
    b = np.arange(bins // 64)[:, None]
    i = (np.arange(8)[None, :] - r) % 8
    return 64 * b + 8 * i + r


def forward_tables(samples):
    bins = samples // 4
    u = np.arange(samples // NBLK)
    tables = []
    for r in range(8):
        f = class_bins(r, bins)[:, :, None]
        angle = 2.0 * np.pi * ((f * u) % samples) / samples
        tables.append(np.stack([np.cos(angle), -np.sin(angle)]).reshape(bins // 4, -1))
    return np.concatenate(tables, 0).astype(ml_dtypes.bfloat16)


def inverse_tables(samples, channels):
    bins = samples // 4
    g = np.arange(bins // 8)[:, None]
    q = np.arange(samples // 8)[None, :]
    angle = 2.0 * np.pi * ((8 * g * q) % samples) / samples
    exact = np.concatenate([np.cos(angle), np.sin(angle)], 1)
    high = exact.astype(ml_dtypes.bfloat16)
    first = np.stack([high, (exact - high.astype(np.float64)).astype(ml_dtypes.bfloat16)])
    r = np.arange(8)[:, None]
    weight = 2.0 / (samples * math.sqrt(channels))
    angle = 2.0 * np.pi * r * q / samples
    twiddle = (weight * np.stack([np.cos(angle), np.sin(angle)])).astype(np.float32)
    p = np.arange(8)[:, None]
    angle = 2.0 * np.pi * ((p * r.T) % 8) / 8
    last = np.concatenate([np.cos(angle), -np.sin(angle)], 1).astype(np.float32)
    return first, twiddle, last


def band_place(edges_ref, first, channels):
    band = jnp.int32(0)
    cut = jnp.int32(channels)
    for e in range(edges_ref.shape[0]):
        edge = edges_ref[e]
        band = band + (edge <= first).astype(jnp.int32)
        cut = jnp.where(edge > first, jnp.minimum(cut, edge), cut)
    return band, cut


def power_kernel(
    group, edges_hbm, keep_hbm, delays_hbm, x_hbm, out_ref, info_ref,
    x_ref, mask_ref, edges_ref, keep_ref, delays_ref, sems, x_sems,
):
    local = x_ref.shape[0]
    window = x_ref.shape[1] // NBLK
    parts = x_sems.shape[0]
    step = local // parts
    channels = local * group
    small = [
        pltpu.make_async_copy(source, target, sems.at[n])
        for n, (source, target) in enumerate(((edges_hbm, edges_ref), (keep_hbm, keep_ref), (delays_hbm, delays_ref)))
    ]
    large = [
        pltpu.make_async_copy(x_hbm.at[pl.ds(n * step, step)], x_ref.at[pl.ds(n * step, step)], x_sems.at[n])
        for n in range(parts)
    ]
    for copy in small + large:
        copy.start()
    for copy in small:
        copy.wait()
    first = lax.axis_index("wide") * local
    band = jnp.int32(0)
    cut = jnp.int32(channels)
    edges = edges_ref.shape[0]
    for e in range(edges):
        edge = edges_ref[e]
        band = band + (edge <= first).astype(jnp.int32)
        cut = jnp.where(edge > first, jnp.minimum(cut, edge), cut)
    ids = first + lax.broadcasted_iota(jnp.int32, (1, local), 1)
    keep = keep_ref[...].astype(F32)
    masks = [jnp.where(inside, keep, 0.0) for inside in (ids < cut, ids >= cut)]
    for j in range(2):
        mask_ref[j] = jnp.broadcast_to(masks[j], (128, local)).T

    wide = info_ref.shape[1]
    lane = lax.broadcasted_iota(jnp.int32, (2 * NBLK, wide), 1)
    row = lax.broadcasted_iota(jnp.int32, (2 * NBLK, wide), 0)
    place = lane == band * NBLK + row
    info_ref[: 2 * NBLK, :] = jnp.where(place, 1.0, 0.0)
    width = jnp.ones((8, wide), F32)
    for j in range(edges + 1):
        low = edges_ref[j - 1] if j else jnp.int32(0)
        high = edges_ref[j] if j < edges else jnp.int32(channels)
        width = jnp.where((lane[:8] >> 3) == j, (high - low).astype(F32), width)
    info_ref[2 * NBLK : HEAD, :] = width
    delay = jnp.zeros((8, wide), F32)
    for d in range(delays_ref.shape[0]):
        delay = jnp.where((lane[:8] >> 3) == d, delays_ref[d].astype(F32), delay)
    info_ref[HEAD:, :] = delay
    for j in range(2):
        info_ref[HEAD + j : HEAD + j + 1, :local] = masks[j]

    totals = [[jnp.zeros((16, 128), F32) for _ in range(NBLK)] for _ in range(2)]
    for n in range(parts):
        large[n].wait()
        for c in range(n * step, (n + 1) * step, 16):
            for k in range(NBLK):
                squares = jnp.zeros((16, 128), F32)
                for u in range(k * window, (k + 1) * window, 128):
                    v = x_ref[c : c + 16, u : u + 128].astype(F32)
                    squares = squares + v * v
                for j in range(2):
                    totals[j][k] = totals[j][k] + squares * mask_ref[j, c : c + 16, :]
    flat = jnp.concatenate([jnp.sum(t, axis=0, keepdims=True) for row in totals for t in row], axis=0)
    sums = jnp.sum(flat, axis=1, keepdims=True) * (1.0 / window)
    lanes = out_ref.shape[1]
    placed = jnp.where(place[:, :lanes], jnp.broadcast_to(sums, (2 * NBLK, lanes)), 0.0)
    out_ref[...] = jnp.broadcast_to(jnp.sum(placed, axis=0, keepdims=True), out_ref.shape)


def turned(a, b):
    return a[0] * b[0] - a[1] * b[1], a[1] * b[0] + a[0] * b[1]


def phase_kernel(group, info_ref, x_hbm, pack_ref, x_ref, sem):
    local, samples = x_ref.shape
    lanes = pack_ref.shape[1]
    channels = local * group
    copy = pltpu.make_async_copy(x_hbm, x_ref, sem)
    copy.start()
    first = lax.axis_index("wide") * local
    pack_ref[:HEAD, :] = info_ref[:HEAD, :lanes]
    for j in range(2):
        mask = jnp.broadcast_to(info_ref[HEAD + j : HEAD + j + 1, :local], (lanes, local))
        pack_ref[HEAD + j * local : HEAD + (j + 1) * local, :] = mask.T
    lane = lax.broadcasted_iota(jnp.int32, (16, lanes), 1)
    delay = jnp.broadcast_to(info_ref[HEAD + 2 : HEAD + 3, :lanes], (16, lanes))
    bins = ((3.5 + 8.0 * (lane & 7).astype(F32)) * delay, 64.0 * delay, 0.5 * delay)

    def rows(n, carry):
        c = pl.multiple_of(n * 16, 16)
        channel = first + c + lax.broadcasted_iota(jnp.int32, (16, lanes), 0)
        ratio = 0.5 + 0.5 * (channel.astype(F32) + 0.5) / channels
        fraction = (1.0 / (ratio * ratio) - 1.0) / 3.0 / samples
        for m in range(3):
            for q, v in enumerate(cos_sin_cycles(bins[m] * fraction)):
                pack_ref[pl.ds(pl.multiple_of(HEAD + (2 + 2 * m + q) * local + c, 8), 16), :] = v
        return carry

    lax.fori_loop(0, local // 16, rows, 0, unroll=2)
    copy.wait()


def window_classes(y):
    half = math.sqrt(0.5)
    e = [y[k] + y[k + 4] for k in range(4)]
    o = [y[k] - y[k + 4] for k in range(4)]
    a, b = e[0] + e[2], e[1] + e[3]
    p, q = half * (o[1] - o[3]), half * (o[1] + o[3])
    return [a + b, a - b, o[0] + p, -(o[2] + q), e[0] - e[2], e[3] - e[1], o[0] - p, o[2] - q]


def main_kernel(
    power_ref, x_ref, pack_ref, table_hbm,
    out_ref, table_ref, z_ref, spec_ref, state_ref, step_ref, part_ref, table_sems,
):
    local, samples = x_ref.shape
    window = samples // NBLK
    lanes = pack_ref.shape[1]
    rows = table_ref.shape[0] // 8
    head = HEAD + 2 * local
    table_copies = [
        pltpu.make_async_copy(
            table_hbm.at[pl.ds(n * rows, rows)], table_ref.at[pl.ds(n * rows, rows)], table_sems.at[n]
        )
        for n in range(8)
    ]
    for n in range(8):
        table_copies[n].start()
    power = jnp.sum(power_ref[...], axis=0, keepdims=True)
    wide = power.shape[1]
    inverse = 1.0 / jnp.sqrt(power / pack_ref[2 * NBLK : 2 * NBLK + 1, :wide] + 1e-05)
    column = jnp.sum(pack_ref[: 2 * NBLK, :wide] * inverse, axis=1, keepdims=True)
    column = jnp.broadcast_to(column, (2 * NBLK, 128))
    scale = [
        [jnp.broadcast_to(column[j * NBLK + k : j * NBLK + k + 1, :], (16, 128)) for k in range(NBLK)]
        for j in range(2)
    ]

    waiting = []

    def store(next_stores):
        for ref, index, value in waiting:
            ref[index] = value
        waiting[:] = next_stores

    for c in range(0, local, 16):
        at = slice(c, c + 16)
        m0 = pack_ref[HEAD + c : HEAD + c + 16, :128]
        m1 = pack_ref[HEAD + local + c : HEAD + local + c + 16, :128]
        weight = [m0 * scale[0][k] + m1 * scale[1][k] for k in range(NBLK)]
        for u in range(0, window, 128):
            y = [x_ref[at, k * window + u : k * window + u + 128].astype(F32) * weight[k] for k in range(NBLK)]
            classes = window_classes(y)
            classes += [-classes[m] for m in (3, 5, 7)]
            store([
                (z_ref, (at, slice(m * window + u, m * window + u + 128)), z.astype(BF16))
                for m, z in enumerate(classes)
            ])
    store([])

    blocks = rows // 16
    contract = (((1,), (1,)), ((), ()))

    def put(r, real, imag):
        j, at = (r - 4, 0) if r >= 4 else (3 - r, 16)
        both = jnp.concatenate([v.reshape(blocks, 8, local) for v in (real, imag)], axis=1)
        spec_ref[j, :, at : at + 16, :] = both.astype(BF16)

    def across(table, n):
        return lax.dot_general(table, n, contract, preferred_element_type=F32)

    half = rows // 2
    for r in (0, 4):
        table_copies[r].wait()
        at = r // 4 * window
        found = across(table_ref[r * rows : (r + 1) * rows, :], z_ref[:, at : at + window])
        put(r, found[:half], found[half:])
    for r in (1, 2, 3):
        table_copies[r].wait()
        table_copies[8 - r].wait()
        real, imag, minus = (z_ref[:, n * window : (n + 1) * window] for n in (2 * r, 2 * r + 1, 7 + r))
        (cos_a, sin_a), (cos_b, sin_b) = (
            (table_ref[n * rows : n * rows + half, :], table_ref[n * rows + half : (n + 1) * rows, :]) for n in (r, 8 - r)
        )
        left = [jnp.concatenate(pair, axis=1) for pair in ((sin_a, cos_a), (cos_b, sin_b))]
        plus = across(jnp.concatenate(left, axis=0), jnp.concatenate([real, imag], axis=1))
        left = [jnp.concatenate(pair, axis=1) for pair in ((cos_a, sin_a), (sin_b, cos_b))]
        other = across(jnp.concatenate(left, axis=0), jnp.concatenate([real, minus], axis=1))
        put(r, other[:half], plus[:half])
        put(8 - r, plus[half:], other[half:])

    def phase(m, at):
        return pack_ref[head + m * local + at.start : head + m * local + at.stop, :]

    for c in range(0, local, 16):
        at = slice(c, c + 16)
        step = phase(4, at), phase(5, at)
        one = turned(step, step)
        stores = [(state_ref, (q, at, slice(None)), phase(q, at)) for q in range(2)]
        for j in range(4):
            stores += [(step_ref, (j, q, at, slice(None)), step[q].astype(BF16)) for q in range(2)]
            step = turned(step, one)
        store(stores)
    store([])

    sub = lax.broadcasted_iota(jnp.int32, (8, lanes), 0)
    inner = lax.broadcasted_iota(jnp.int32, (8, lanes), 1) & 7
    skew = (sub - inner) & 7

    def generate(count):
        made = []
        for c in range(0, local, 16):
            at = slice(c, c + 16)
            state = state_ref[0, at, :], state_ref[1, at, :]
            turn = phase(2, at), phase(3, at)
            steps = [(step_ref[j, 0, at, :], step_ref[j, 1, at, :]) for j in range(4)]
            products = []
            for _ in range(count):
                cos0, sin0 = (v.astype(BF16) for v in state)
                for cos_j, sin_j in steps:
                    cc, ss, sc, cs = cos0 * cos_j, sin0 * sin_j, sin0 * cos_j, cos0 * sin_j
                    for pair in ((cc - ss, sc + cs), (cc + ss, sc - cs)):
                        products.append(jnp.concatenate(pair, axis=1))
                state = turned(state, turn)
            made.append(products)
            store([(state_ref, (q, at, slice(None)), state[q]) for q in range(2)])
        store([])
        return [
            [jnp.concatenate([products[8 * n + m] for products in made], axis=0) for m in range(8)] for n in range(count)
        ]

    def dedisperse(b, tiles):
        found = [None] * 8
        for j in range(4):
            both = spec_ref[j, b]
            up = jnp.dot(both[:16], tiles[2 * j], preferred_element_type=F32)
            down = jnp.dot(both[16:], tiles[2 * j + 1], preferred_element_type=F32)
            cos_up, sin_up, cos_down, sin_down = up[:, :lanes], up[:, lanes:], down[:, :lanes], down[:, lanes:]
            found[4 + j] = cos_up[:8] - sin_up[8:], sin_up[:8] + cos_up[8:]
            found[3 - j] = cos_down[:8] - sin_down[8:], sin_down[:8] + cos_down[8:]
        real, imag = found[0]
        for r in range(1, 8):
            real = jnp.where(skew == r, found[r][0], real)
            imag = jnp.where(skew == r, found[r][1], imag)
        for bit in (1, 2, 4):
            move = (inner & bit) != 0
            real = jnp.where(move, pltpu.roll(real, 8 - bit, 0), real)
            imag = jnp.where(move, pltpu.roll(imag, 8 - bit, 0), imag)
        part_ref[0, b] = real
        part_ref[1, b] = imag

    def several(n, carry):
        for m, tiles in enumerate(generate(AT_ONCE)):
            dedisperse(n * AT_ONCE + m, tiles)
        return carry

    lax.fori_loop(0, blocks // AT_ONCE, several, 0, unroll=8)

    block = lax.broadcasted_iota(jnp.int32, (8, 128), 1) >> 3
    for half in range(lanes // 128):
        done = []
        for part in range(2):
            v = [part_ref[part, b, :, half * 128 : half * 128 + 128] for b in range(16)]
            for bit in (1, 2, 4, 8):
                w = list(v)
                high = (block & bit) != 0
                for b in range(16):
                    if b & bit:
                        w[b] = jnp.where(high, v[b], pltpu.roll(v[b ^ bit], 128 - 8 * bit, 1))
                    else:
                        w[b] = jnp.where(high, pltpu.roll(v[b ^ bit], 8 * bit, 1), v[b])
                v = w
            done.append(v)
        for d in range(16):
            out_ref[half * 16 + d] = jnp.concatenate([done[0][d], done[1][d]], axis=0).astype(BF16)


def inverse_kernel(group, got_ref, first_ref, twiddle_ref, last_ref, out_ref):
    step = first_ref.shape[2] // 2
    trials = out_ref.shape[1]
    row = lax.broadcasted_iota(jnp.int32, (16, 128), 0)
    lane = lax.broadcasted_iota(jnp.int32, (16, 128), 1)
    dc = ((row & 7) == 0) & (lane == 0)
    for d in range(trials):
        total = got_ref[d].astype(F32)
        for n in range(1, group):
            total = total + got_ref[n * trials + d].astype(F32)
        total = jnp.where(dc, 0.5 * total, total)
        high = total.astype(BF16)
        low = (total - high.astype(F32)).astype(BF16)
        y = jnp.dot(jnp.concatenate([high, low], axis=0), first_ref[0], preferred_element_type=F32)
        y = y[:16] + y[16:] + jnp.dot(high, first_ref[1], preferred_element_type=F32)
        real = y[0:8, :step] - y[8:16, step:]
        imag = y[0:8, step:] + y[8:16, :step]
        cos, sin = twiddle_ref[0], twiddle_ref[1]
        z = jnp.concatenate([real * cos - imag * sin, real * sin + imag * cos], axis=0)
        series = jnp.dot(last_ref[...], z, precision=lax.Precision.HIGHEST, preferred_element_type=F32)
        for p in range(8):
            out_ref[0, d : d + 1, p * step : (p + 1) * step] = series[p : p + 1, :]


def call(kernel, out_shape, in_specs, scratch=(), vmem=52000, name=None):
    return pl.pallas_call(
        kernel,
        out_shape=out_shape,
        in_specs=in_specs,
        out_specs=jax.tree.map(lambda _: VMEM, out_shape),
        scratch_shapes=list(scratch),
        compiler_params=pltpu.CompilerParams(vmem_limit_bytes=vmem * 2**10),
        name=name,
    )


def body(filterbank, channel_mask, band_edges, dm_delays):
    _, local, samples = filterbank.shape
    group = lax.axis_size("wide")
    channels = local * group
    trials = dm_delays.shape[0]
    lanes = 8 * trials
    bins = samples // 4
    blocks = bins // 64
    shape = jax.ShapeDtypeStruct
    x = filterbank.reshape(local, samples)
    keep = channel_mask.reshape(1, local)
    power_lanes = -(-(band_edges.shape[0] + 1) * NBLK // 128) * 128
    edges_scratch = pltpu.SMEM(band_edges.shape, jnp.int32)
    keep_scratch = pltpu.VMEM(keep.shape, jnp.int32)

    power, info = call(
        functools.partial(power_kernel, group),
        (shape((group, power_lanes), F32), shape((HEAD + 8, max(local, lanes)), F32)),
        [HBM] * 4,
        [
            pltpu.VMEM((local, samples), BF16),
            pltpu.VMEM((2, local, 128), F32),
            edges_scratch,
            keep_scratch,
            pltpu.SMEM(dm_delays.shape, jnp.int32),
            pltpu.SemaphoreType.DMA((3,)),
            pltpu.SemaphoreType.DMA((4,)),
        ],
        vmem=65536,
        name="band_power",
    )(band_edges, keep, dm_delays, x)
    all_power = lax.all_to_all(power, "wide", 0, 0, tiled=True)

    pack, x = call(
        functools.partial(phase_kernel, group),
        (shape((HEAD + 8 * local, lanes), F32), shape((local, samples), BF16)),
        [VMEM, HBM],
        [pltpu.SemaphoreType.DMA],
        name="phases",
    )(info, x)

    table = forward_tables(samples)
    partial = call(
        main_kernel,
        shape((trials, 16, 128), BF16),
        [VMEM] * 3 + [HBM],
        [
            pltpu.VMEM(table.shape, BF16),
            pltpu.VMEM((local, 11 * samples // 8), BF16),
            pltpu.VMEM((4, blocks, 32, local), BF16),
            pltpu.VMEM((2, local, lanes), F32),
            pltpu.VMEM((4, 2, local, lanes), BF16),
            pltpu.VMEM((2, blocks, 8, lanes), F32),
            pltpu.SemaphoreType.DMA((8,)),
        ],
        name="dedisperse",
    )(all_power, x, pack, jnp.asarray(table))
    got = lax.all_to_all(partial, "wide", 0, 0, tiled=True)

    first, twiddle, last = inverse_tables(samples, channels)
    return call(
        functools.partial(inverse_kernel, group),
        shape((1, trials // group, samples), F32),
        [VMEM] * 4,
        vmem=8192,
        name="inverse",
    )(got, jnp.asarray(first), jnp.asarray(twiddle), jnp.asarray(last))


def solution(mesh):
    return jax.shard_map(
        body,
        mesh=mesh,
        in_specs=(P("beam", "wide", None), P(("beam", "wide")), P(), P()),
        out_specs=P("beam", "wide", None),
        check_vma=False,
    )
```
